32 devices in a mesh: gx: 4 (over x, core), gy: 8 (over z, y).
Axes of the slice: x: 2, y: 2, z: 4, core: 2. Of those that a mesh axis runs over, the one named last changes fastest.
Arguments:
- phase_field: float32 [16, 2048, 2048], P(None, 'gy', 'gx'), may hold values from -1 to 1
- mobility: float32 [16, 2048, 2048], P(None, 'gy', 'gx'), may hold values from 0.25 to 2.5
- x_inverse: bfloat16 [2048, 2048], P('gx'), may hold values from -2 to 2
- y_inverse: bfloat16 [2048, 2048], P('gy'), may hold values from -2 to 2
Outputs:
- new_phase: float32 [16, 2048, 2048], P(None, 'gy', 'gx')
The draws below stay inside these ranges and needn't reach their ends.
All inputs are finite; a program needn't handle non-finite values.
Results may differ from the reference program's by a relative error of at most 0.0041.
Values may be sent and summed in bfloat16 or wider, within the bound.
A program may use at most 128 MiB of HBM per device.

```python
import math
import jax
import jax.numpy as jnp
from jax import lax

NX = 2048
NY = 2048
PZ = 16
CX = 512
CY = 256


def line_inverse(key, order, reach):
    index = jnp.arange(order)
    distance = jnp.abs(index[:, None] - index[None, :]).astype(jnp.float32)
    envelope = jnp.exp(-distance / reach)
    noise = jnp.clip(jax.random.normal(jax.random.fold_in(key, 11), (order, order), jnp.float32), -4.0, 4.0)
    far_noise = jnp.clip(jax.random.normal(jax.random.fold_in(key, 13), (order, order), jnp.float32), -4.0, 4.0)
    diagonal = jax.random.uniform(jax.random.fold_in(key, 12), (order,), jnp.float32, 0.4, 0.8)
    matrix = jnp.diag(diagonal) + 0.5 * noise * envelope / jnp.sqrt(2.0 * reach)
    matrix = matrix + 0.6 * far_noise / jnp.sqrt(1.0 * order)
    return matrix.astype(jnp.bfloat16)


def draw_x_inverse(key, part):
    return line_inverse(jax.random.fold_in(key, 1), NX, 2.0 * CX)


def draw_y_inverse(key, part):
    return line_inverse(jax.random.fold_in(key, 2), NY, 2.0 * CY)


def block_levels(rng, extent, cuts, least, high):
    def one(position, blocks):
        steps = jax.random.uniform(jax.random.fold_in(jax.random.fold_in(rng, 6), position), (blocks,), jnp.float32, least / len(cuts), high / len(cuts))
        return jnp.repeat(jnp.exp(steps), extent[position] // blocks).reshape((-1,) + (1,) * (len(extent) - position - 1))

    factor_of = one(*cuts[0])
    for cut in cuts[1:]:
        factor_of = factor_of * one(*cut)
    return factor_of


def setup_inputs(seed: int = 0) -> dict:
    seeds = jax.random.split(jax.random.key(seed), 5)
    phase_field = jnp.clip(jax.random.uniform(seeds[0], (PZ, NY, NX), jnp.float32, -1.0, 1.0) * block_levels(seeds[0], (PZ, NY, NX), ((1, 8), (2, 4)), -0.4, 0.0), -1.0, 1.0)
    mobility = jnp.clip(jnp.exp(math.log(2.5) - 2.3025851 * jax.random.uniform(seeds[1], (PZ, NY, NX), jnp.float32) ** block_levels(seeds[1], (PZ, NY, NX), ((1, 8), (2, 4)), -0.2, 0.2)), 0.25, 2.5)
    x_inverse = draw_x_inverse(jax.random.fold_in(seeds[4], 71), 0)
    y_inverse = draw_y_inverse(jax.random.fold_in(seeds[4], 71), 0)
    return {"phase_field": phase_field, "mobility": mobility, "x_inverse": x_inverse, "y_inverse": y_inverse}


step_size = 0.15


def face_mob(center_mob, near_mob):
    return 2.0 * center_mob * near_mob / jnp.maximum(center_mob + near_mob, 0.25)


def laplace(values, mobile):
    values_z = jnp.pad(values, ((1, 1), (0, 0), (0, 0)))
    mobile_z = jnp.pad(mobile, ((1, 1), (0, 0), (0, 0)))
    center = values[:, 1:-1, 1:-1]
    center_mob = mobile[:, 1:-1, 1:-1]
    pairs = [
        (values_z[2:, 1:-1, 1:-1], mobile_z[2:, 1:-1, 1:-1]),
        (values_z[:-2, 1:-1, 1:-1], mobile_z[:-2, 1:-1, 1:-1]),
        (values[:, 2:, 1:-1], mobile[:, 2:, 1:-1]),
        (values[:, :-2, 1:-1], mobile[:, :-2, 1:-1]),
        (values[:, 1:-1, 2:], mobile[:, 1:-1, 2:]),
        (values[:, 1:-1, :-2], mobile[:, 1:-1, :-2]),
    ]
    result = jnp.zeros_like(center)
    for near_val, near_mob in pairs:
        result = result + face_mob(center_mob, near_mob) * (near_val - center)
    return result


def pad_yx(array):
    return jnp.pad(array, ((0, 0), (1, 1), (1, 1)))


def reference(phase_field, mobility, x_inverse, y_inverse):
    mob_pad = pad_yx(mobility)
    first = phase_field + step_size * laplace(pad_yx(phase_field), mob_pad)
    second = (first + step_size * laplace(pad_yx(first), mob_pad)).astype(jnp.bfloat16)

    def solve_x(plane):
        return jnp.dot(plane, x_inverse.T, preferred_element_type=jnp.float32)

    solved = lax.map(solve_x, second)
    chemical = solved * solved * solved - solved
    updated = (solved + step_size * laplace(pad_yx(chemical), mob_pad)).astype(jnp.bfloat16)

    def solve_y(plane):
        return jnp.dot(y_inverse, plane, preferred_element_type=jnp.float32)

    return lax.map(solve_y, updated)
```

```python
import functools

import jax
import jax.numpy as jnp
from jax import lax
from jax.experimental import pallas as pl
from jax.experimental.pallas import tpu as pltpu
from jax.sharding import PartitionSpec as P

step_size = 0.15
PAD = 8
STRIP = 32
MESH = pl.DeviceIdType.MESH


def face_mob(center_mob, near_mob):
    return 2.0 * center_mob * near_mob / jnp.maximum(center_mob + near_mob, 0.25)


def extended(x, sides, width):
    for axis, dim in sides:
        size, length = (lax.axis_size(axis), x.shape[dim])
        up = [(i, (i + 1) % size) for i in range(size - 1)]
        down = [(j, i) for i, j in up]
        last = lax.slice_in_dim(x, length - width, length, axis=dim)
        leading = lax.slice_in_dim(x, 0, width, axis=dim)
        before = lax.ppermute(last, axis, up)
        after = lax.ppermute(leading, axis, down)
        x = jnp.concatenate([before, x, after], axis=dim)
    return x


def laplace(values, mobile):
    values_z = jnp.pad(values, ((1, 1), (0, 0), (0, 0)))
    mobile_z = jnp.pad(mobile, ((1, 1), (0, 0), (0, 0)))
    center = values[:, 1:-1, 1:-1]
    center_mob = mobile[:, 1:-1, 1:-1]
    pairs = [
        (values_z[2:, 1:-1, 1:-1], mobile_z[2:, 1:-1, 1:-1]),
        (values_z[:-2, 1:-1, 1:-1], mobile_z[:-2, 1:-1, 1:-1]),
        (values[:, 2:, 1:-1], mobile[:, 2:, 1:-1]),
        (values[:, :-2, 1:-1], mobile[:, :-2, 1:-1]),
        (values[:, 1:-1, 2:], mobile[:, 1:-1, 2:]),
        (values[:, 1:-1, :-2], mobile[:, 1:-1, :-2]),
    ]
    result = jnp.zeros_like(center)
    for near_val, near_mob in pairs:
        result = result + face_mob(center_mob, near_mob) * (near_val - center)
    return result


def plain(phase_field, mobility, x_inverse, y_inverse):
    whole_inverse = lax.all_gather(y_inverse, "gy", axis=0, tiled=True)
    stacked = jnp.stack((phase_field, mobility))
    padded = extended(stacked, (("gx", 3), ("gy", 2)), 1)
    mob_near = padded[1]
    first = phase_field + step_size * laplace(padded[0], mob_near)
    first_pad = extended(first, (("gx", 2), ("gy", 1)), 1)
    second = (first + step_size * laplace(first_pad, mob_near)).astype(jnp.bfloat16)
    planes, y_rows, x_rows = second.shape
    out_rows = x_inverse.shape[0]
    segment = lax.all_gather(second, "gx", axis=2, tiled=True)
    flat = segment.reshape(planes * y_rows, segment.shape[2])
    lines = lax.dot_general(
        flat, x_inverse, (((1,), (1,)), ((), ())), preferred_element_type=jnp.float32
    )
    solved = lines.reshape(planes, y_rows, out_rows)
    chemical = solved * solved * solved - solved
    chemical_pad = extended(chemical, (("gx", 2), ("gy", 1)), 1)
    updated = (solved + step_size * laplace(chemical_pad, mob_near)).astype(jnp.bfloat16)
    columns = jnp.transpose(updated, (1, 0, 2)).reshape(y_rows, planes * x_rows)
    line_block = lax.all_to_all(columns, "gy", split_axis=1, concat_axis=0, tiled=True)
    solved_cols = jnp.dot(whole_inverse, line_block, preferred_element_type=jnp.float32)
    returned = lax.all_to_all(solved_cols, "gy", split_axis=0, concat_axis=1, tiled=True)
    return jnp.transpose(returned.reshape(y_rows, planes, x_rows), (1, 0, 2))


def strip_laplace(v, m, v_below, m_below, flux_above, v_cols, m_cols):
    rows, width = v.shape
    own = slice(PAD, rows - PAD)
    flux = face_mob(m, pltpu.roll(m, rows - 1, 0)) * (pltpu.roll(v, rows - 1, 0) - v)
    total = flux[own] - pltpu.roll(flux, 1, 0)[own]
    v, m = v[own], m[own]
    flux_below = face_mob(m, m_below) * (v_below - v)
    total = total + (flux_below - flux_above)
    lane = lax.broadcasted_iota(jnp.int32, v.shape, 1)
    at_end = lane == width - 1
    v_next = jnp.where(at_end, v_cols[:, 1:2], pltpu.roll(v, width - 1, 1))
    m_next = jnp.where(at_end, m_cols[:, 1:2], pltpu.roll(m, width - 1, 1))
    flux = face_mob(m, m_next) * (v_next - v)
    entering = face_mob(m_cols[:, 0:1], m[:, 0:1]) * (v[:, 0:1] - v_cols[:, 0:1])
    total = total + (flux - jnp.where(lane == 0, entering, pltpu.roll(flux, 1, 1)))
    return total, flux_below


def explicit_kernel(v_hbm, v_up, v_down, m_hbm, m_up, m_down, v_cols, m_cols, out_ref, v, m, above, sems):
    planes, y_rows, width = v_hbm.shape

    def copies(z):
        out = []
        for k, (src, up, down, dst) in enumerate(((v_hbm, v_up, v_down, v), (m_hbm, m_up, m_down, m))):
            out.append(pltpu.make_async_copy(src.at[z], dst.at[z, pl.ds(PAD, y_rows), :], sems.at[z, 3 * k]))
            out.append(pltpu.make_async_copy(up.at[z], dst.at[z, pl.ds(0, PAD), :], sems.at[z, 3 * k + 1]))
            out.append(pltpu.make_async_copy(down.at[z], dst.at[z, pl.ds(PAD + y_rows, PAD), :], sems.at[z, 3 * k + 2]))
        return out

    @pl.loop(0, planes)
    def _(z):
        for copy in copies(z):
            copy.start()

    v[planes] = jnp.zeros(v.shape[1:], v.dtype)
    m[planes] = jnp.zeros(m.shape[1:], m.dtype)
    above[...] = jnp.zeros_like(above)
    for copy in copies(0):
        copy.wait()

    @pl.loop(0, planes)
    def _(z):
        @pl.when(z + 1 < planes)
        def _():
            for copy in copies(z + 1):
                copy.wait()

        @pl.loop(0, y_rows // STRIP)
        def _(i):
            r = pl.multiple_of(i * STRIP, STRIP)
            near = pl.ds(r, STRIP + 2 * PAD)
            inner = pl.ds(r + PAD, STRIP)
            mine = pl.ds(r, STRIP)
            total, below = strip_laplace(
                v[z, near, :], m[z, near, :], v[z + 1, inner, :], m[z + 1, inner, :],
                above[mine, :], v_cols[z, mine, :], m_cols[z, mine, :],
            )
            above[mine, :] = below
            out_ref[z, mine, :] = (v[z, inner, :] + step_size * total).astype(out_ref.dtype)


def explicit_step(v, v_halo, m, m_halo, dtype):
    planes, y_rows, width = v.shape
    tall = pltpu.VMEM((planes + 1, y_rows + 2 * PAD, width), jnp.float32)
    any_spec, vmem_spec = pl.BlockSpec(memory_space=pl.ANY), pl.BlockSpec(memory_space=pltpu.VMEM)
    return pl.pallas_call(
        explicit_kernel,
        out_shape=jax.ShapeDtypeStruct(v.shape, dtype),
        in_specs=[any_spec] * 6 + [vmem_spec] * 2,
        out_specs=vmem_spec,
        scratch_shapes=[tall, tall, pltpu.VMEM((y_rows, width), jnp.float32), pltpu.SemaphoreType.DMA((planes, 6))],
        compiler_params=pltpu.CompilerParams(vmem_limit_bytes=48 * 2**20),
        cost_estimate=pl.CostEstimate(flops=60 * v.size, bytes_accessed=14 * v.size, transcendentals=0),
    )(v, v_halo[0], v_halo[1], m, m_halo[0], m_halo[1], v_halo[2], m_halo[2])


def solve_kernel(
    nx, ny, stages, w,
    second, m_hbm, m_up, m_down, m_cols, x_cols, y_hbm, out,
    gath, xt, yinv, solved, edge, m, above, upd, yrecv,
    load_sems, own_sems, gx_send, gx_recv, pair_send, pair_recv, row_send, row_recv,
    a2a_send, a2a_recv, ret_send, ret_recv, keep_sems,
):
    planes, y_rows, width = second.shape
    gx, gy = lax.axis_index("gx"), lax.axis_index("gy")
    partner = gx + 1 - 2 * lax.rem(gx, 2)
    half = nx // 2
    per = len(stages)
    chunk = planes // per
    cuts = width // w

    barrier = pltpu.get_barrier_semaphore()
    for d in range(1, ny):
        pl.semaphore_signal(barrier, inc=1, device_id=(gx, lax.rem(gy + d, ny)), device_id_type=MESH)
    for d in range(1, half):
        pl.semaphore_signal(barrier, inc=1, device_id=(lax.rem(gx + 2 * d, nx), gy), device_id_type=MESH)
    pl.semaphore_signal(barrier, inc=1, device_id=(partner, gy), device_id_type=MESH)

    loads = [
        pltpu.make_async_copy(x_cols, xt, load_sems.at[0]),
        pltpu.make_async_copy(m_hbm, m.at[pl.ds(0, planes), pl.ds(PAD, y_rows), :], load_sems.at[1]),
        pltpu.make_async_copy(m_up, m.at[pl.ds(0, planes), pl.ds(0, PAD), :], load_sems.at[2]),
        pltpu.make_async_copy(m_down, m.at[pl.ds(0, planes), pl.ds(PAD + y_rows, PAD), :], load_sems.at[3]),
        pltpu.make_async_copy(y_hbm, yinv, load_sems.at[4]),
    ]

    def own(s):
        lo, n = stages[s]
        return pltpu.make_async_copy(second.at[pl.ds(lo, n)], gath.at[gx, pl.ds(lo, n)], own_sems.at[s])

    def across(s, d):
        lo, n = stages[s]
        return pltpu.make_async_remote_copy(
            second.at[pl.ds(lo, n)], gath.at[gx, pl.ds(lo, n)], gx_send.at[s, d], gx_recv.at[s, d],
            device_id=(lax.rem(gx + 2 * d, nx), gy), device_id_type=MESH)

    def arrived(s, d):
        lo, n = stages[s]
        slot = lax.rem(gx - 2 * d + nx, nx)
        return pltpu.make_async_remote_copy(
            second.at[pl.ds(lo, n)], gath.at[slot, pl.ds(lo, n)], gx_send.at[s, d], gx_recv.at[s, d],
            device_id=(lax.rem(gx + 2 * d, nx), gy), device_id_type=MESH)

    def to_pair(s, d):
        lo, n = stages[s]
        slot = lax.rem(gx - 2 * d + nx, nx)
        src = second.at[pl.ds(lo, n)] if d == 0 else gath.at[slot, pl.ds(lo, n)]
        return pltpu.make_async_remote_copy(
            src, gath.at[slot, pl.ds(lo, n)], pair_send.at[s, d], pair_recv.at[s, d],
            device_id=(partner, gy), device_id_type=MESH)

    def from_pair(s, d):
        lo, n = stages[s]
        slot = lax.rem(partner - 2 * d + nx, nx)
        return pltpu.make_async_remote_copy(
            second.at[pl.ds(lo, n)], gath.at[slot, pl.ds(lo, n)], pair_send.at[s, d], pair_recv.at[s, d],
            device_id=(partner, gy), device_id_type=MESH)

    def rows(s, side):
        lo, n = stages[s]
        src, dst, peer = (PAD, PAD + y_rows, lax.rem(gy + ny - 1, ny)) if side == 0 else (y_rows, 0, lax.rem(gy + 1, ny))
        return pltpu.make_async_remote_copy(
            solved.at[pl.ds(lo, n), pl.ds(src, PAD), :], solved.at[pl.ds(lo, n), pl.ds(dst, PAD), :],
            row_send.at[s, side], row_recv.at[s, side], device_id=(gx, peer), device_id_type=MESH)

    def spread(s, d):
        peer = lax.rem(gy + d, ny)
        return pltpu.make_async_remote_copy(
            upd.at[s, peer], yrecv.at[s, gy], a2a_send.at[s, d], a2a_recv.at[s, d],
            device_id=(gx, peer), device_id_type=MESH)

    def landed(s, d):
        return pltpu.make_async_remote_copy(
            upd.at[s, 0], yrecv.at[s, lax.rem(gy - d + ny, ny)], a2a_send.at[s, d], a2a_recv.at[s, d],
            device_id=(gx, lax.rem(gy + d, ny)), device_id_type=MESH)

    def back(s, d):
        peer = lax.rem(gy + d, ny)
        return pltpu.make_async_remote_copy(
            upd.at[s, peer], out.at[s, gy], ret_send.at[s, d], ret_recv.at[s, d],
            device_id=(gx, peer), device_id_type=MESH)

    def returned(s, d):
        return pltpu.make_async_remote_copy(
            upd.at[s, 0], out.at[s, lax.rem(gy - d + ny, ny)], ret_send.at[s, d], ret_recv.at[s, d],
            device_id=(gx, lax.rem(gy + d, ny)), device_id_type=MESH)

    def keep_in(s):
        return pltpu.make_async_copy(upd.at[s, gy], yrecv.at[s, gy], keep_sems.at[0, s])

    def keep_out(s):
        return pltpu.make_async_copy(upd.at[s, gy], out.at[s, gy], keep_sems.at[1, s])

    for s in range(per):
        own(s).start()
    for copy in loads:
        copy.start()
    pl.semaphore_wait(barrier, ny - 1 + half)
    for s in range(per):
        for d in range(1, half):
            across(s, d).start()
        to_pair(s, 0).start()

    solved[planes] = jnp.zeros(solved.shape[1:], solved.dtype)
    m[planes] = jnp.zeros(m.shape[1:], m.dtype)
    above[...] = jnp.zeros_like(above)

    def solve_x(s):
        lo, n = stages[s]
        for d in range(1, half):
            arrived(s, d).wait_recv()
            to_pair(s, d).start()
        own(s).wait()
        for d in range(half):
            from_pair(s, d).wait_recv()
        if s == 0:
            loads[0].wait()

        @pl.loop(lo, lo + n)
        def _(z):
            total = jnp.zeros((y_rows, xt.shape[2]), jnp.float32)
            for b in range(nx):
                total = total + jnp.dot(gath[b, z], xt[b], preferred_element_type=jnp.float32)
            solved[z, pl.ds(PAD, y_rows), :] = total[:, :width]
            edge[z] = total[:, width:]

        for side in range(2):
            rows(s, side).start()
        if s == 0:
            for copy in loads[1:4]:
                copy.wait()
        for side in range(2):
            rows(s, side).wait_recv()

        @pl.loop(s * chunk, (s + 1) * chunk)
        def _(z):
            @pl.loop(0, y_rows // STRIP)
            def _(i):
                r = pl.multiple_of(i * STRIP, STRIP)
                near = pl.ds(r, STRIP + 2 * PAD)
                inner = pl.ds(r + PAD, STRIP)
                mine = pl.ds(r, STRIP)

                def chemical(u):
                    return u * u * u - u

                tall = solved[z, near, :]
                total, below = strip_laplace(
                    chemical(tall), m[z, near, :], chemical(solved[z + 1, inner, :]), m[z + 1, inner, :],
                    above[mine, :], chemical(edge[z, mine, :]), m_cols[z, mine, :],
                )
                above[mine, :] = below
                value = (tall[PAD:PAD + STRIP] + step_size * total).astype(upd.dtype)
                for c in range(cuts):
                    upd[s, (z - s * chunk) * cuts + c, mine, :] = value[:, c * w:(c + 1) * w]

        keep_in(s).start()

        @pl.loop(1, ny)
        def _(d):
            spread(s, d).start()

    def solve_y(s):
        if s == 0:
            loads[4].wait()
        keep_in(s).wait()

        @pl.loop(1, ny)
        def _(d):
            landed(s, d).wait_recv()
            spread(s, d).wait_send()

        def block(d):
            peer = lax.rem(gy + d, ny)
            lines = yrecv[s].reshape(ny * y_rows, w)
            upd[s, peer] = jnp.dot(
                yinv[pl.ds(pl.multiple_of(peer * y_rows, y_rows), y_rows), :], lines,
                preferred_element_type=jnp.float32).astype(upd.dtype)

        @pl.loop(1, ny)
        def _(d):
            block(d)
            back(s, d).start()

        block(0)
        keep_out(s).start()

    for s in range(per):
        solve_x(s)
        if s > 0:
            solve_y(s - 1)
    solve_y(per - 1)

    for s in range(per):
        for d in range(1, half):
            across(s, d).wait_send()
        for d in range(half):
            to_pair(s, d).wait_send()
        for side in range(2):
            rows(s, side).wait_send()
        keep_out(s).wait()

        @pl.loop(1, ny)
        def _(d):
            back(s, d).wait_send()
            returned(s, d).wait_recv()


def both_solves(second, mobility, m_halo, x_cols, whole_inverse, per):
    planes, y_rows, width = second.shape
    nx, ny = lax.axis_size("gx"), lax.axis_size("gy")
    chunk = planes // per
    w = chunk * width // ny
    ends = [min((s + 1) * chunk + 1, planes) for s in range(per)]
    stages = [(0 if s == 0 else ends[s - 1], ends[s] - (0 if s == 0 else ends[s - 1])) for s in range(per)]
    tall = pltpu.VMEM((planes + 1, y_rows + 2 * PAD, width), jnp.float32)
    extra = x_cols.shape[2] - width
    any_spec, vmem_spec = pl.BlockSpec(memory_space=pl.ANY), pl.BlockSpec(memory_space=pltpu.VMEM)
    dma = pltpu.SemaphoreType.DMA
    bf16 = jnp.bfloat16
    return pl.pallas_call(
        functools.partial(solve_kernel, nx, ny, stages, w),
        out_shape=jax.ShapeDtypeStruct((per, ny, y_rows, w), bf16),
        in_specs=[any_spec] * 4 + [vmem_spec] + [any_spec] * 2,
        out_specs=any_spec,
        scratch_shapes=[
            pltpu.VMEM((nx, planes, y_rows, width), bf16),
            pltpu.VMEM(x_cols.shape, bf16),
            pltpu.VMEM(whole_inverse.shape, bf16),
            tall,
            pltpu.VMEM((planes, y_rows, extra), jnp.float32),
            tall,
            pltpu.VMEM((y_rows, width), jnp.float32),
            pltpu.VMEM((per, ny, y_rows, w), bf16),
            pltpu.VMEM((per, ny, y_rows, w), bf16),
            dma((5,)), dma((per,)),
            dma((per, nx // 2)), dma((per, nx // 2)), dma((per, nx // 2)), dma((per, nx // 2)),
            dma((per, 2)), dma((per, 2)),
            dma((per, ny)), dma((per, ny)), dma((per, ny)), dma((per, ny)),
            dma((2, per)),
        ],
        compiler_params=pltpu.CompilerParams(
            collective_id=0, has_side_effects=True, vmem_limit_bytes=62 * 2**20),
        cost_estimate=pl.CostEstimate(flops=8192 * second.size, bytes_accessed=40 * second.size, transcendentals=0),
    )(second, mobility, m_halo[0], m_halo[1], m_halo[2], x_cols, whole_inverse)


def shifted(x, axis):
    size = lax.axis_size(axis)
    up = [(i, i + 1) for i in range(size - 1)]
    down = [(j, i) for i, j in up]
    return lax.ppermute(x[0], axis, up), lax.ppermute(x[1], axis, down)


def halos(v):
    up, down = shifted((v[:, -PAD:, :], v[:, :PAD, :]), "gy")
    left, right = shifted((v[:, :, -1], v[:, :, 0]), "gx")
    return up, down, jnp.stack((left, right), axis=-1)


def local(per, phase_field, mobility, x_inverse, y_inverse):
    planes, y_rows, width = phase_field.shape
    nx = lax.axis_size("gx")
    whole_inverse = lax.all_gather(y_inverse, "gy", axis=0, tiled=True)
    before, after = shifted((x_inverse[-1:], x_inverse[:1]), "gx")
    spare = jnp.zeros((126, x_inverse.shape[1]), x_inverse.dtype)
    x_cols = jnp.concatenate([x_inverse, before, after, spare], axis=0).T.reshape(nx, width, width + 128)
    m_halo = halos(mobility)
    first = explicit_step(phase_field, halos(phase_field), mobility, m_halo, jnp.float32)
    second = explicit_step(first, halos(first), mobility, m_halo, jnp.bfloat16)
    lines = both_solves(second, mobility, m_halo, x_cols, whole_inverse, per)
    w = lines.shape[3]
    lines = lines.reshape(planes, width // w, y_rows, w)
    return jnp.transpose(lines, (0, 2, 1, 3)).reshape(planes, y_rows, width).astype(jnp.float32)


def chunks(planes, y_rows, width, nx, ny):
    if nx % 2 or nx < 2 or ny < 3 or y_rows % STRIP or width % 128:
        return 0
    if 30 * planes * y_rows * width > 64 * 2**20:
        return 0
    for per in (4, 2, 1):
        if planes % per == 0 and planes // per * width % ny == 0:
            w = planes // per * width // ny
            if w % 128 == 0 and width % w == 0:
                return per
    return 0


def solution(mesh):
    placed = (P(None, "gy", "gx"), P(None, "gy", "gx"), P("gx", None), P("gy", None))
    nx, ny = mesh.shape["gx"], mesh.shape["gy"]

    def step(phase_field, mobility, x_inverse, y_inverse):
        planes, rows, cols = phase_field.shape
        per = chunks(planes, rows // ny, cols // nx, nx, ny)
        body = functools.partial(local, per) if per else plain
        return jax.shard_map(
            body, mesh=mesh, in_specs=placed, out_specs=P(None, "gy", "gx"), check_vma=False
        )(phase_field, mobility, x_inverse, y_inverse)

    return step
```

```python
import functools

import jax
import jax.numpy as jnp
from jax import lax
from jax.experimental import pallas as pl
from jax.experimental.pallas import tpu as pltpu
from jax.sharding import PartitionSpec as P

step_size = 0.15
PAD = 8
STRIP = 32
MESH = pl.DeviceIdType.MESH


def face_mob(center_mob, near_mob):
    return 2.0 * center_mob * near_mob / jnp.maximum(center_mob + near_mob, 0.25)


def extended(x, sides, width):
    for axis, dim in sides:
        size, length = (lax.axis_size(axis), x.shape[dim])
        up = [(i, (i + 1) % size) for i in range(size - 1)]
        down = [(j, i) for i, j in up]
        last = lax.slice_in_dim(x, length - width, length, axis=dim)
        leading = lax.slice_in_dim(x, 0, width, axis=dim)
        before = lax.ppermute(last, axis, up)
        after = lax.ppermute(leading, axis, down)
        x = jnp.concatenate([before, x, after], axis=dim)
    return x


def laplace(values, mobile):
    values_z = jnp.pad(values, ((1, 1), (0, 0), (0, 0)))
    mobile_z = jnp.pad(mobile, ((1, 1), (0, 0), (0, 0)))
    center = values[:, 1:-1, 1:-1]
    center_mob = mobile[:, 1:-1, 1:-1]
    pairs = [
        (values_z[2:, 1:-1, 1:-1], mobile_z[2:, 1:-1, 1:-1]),
        (values_z[:-2, 1:-1, 1:-1], mobile_z[:-2, 1:-1, 1:-1]),
        (values[:, 2:, 1:-1], mobile[:, 2:, 1:-1]),
        (values[:, :-2, 1:-1], mobile[:, :-2, 1:-1]),
        (values[:, 1:-1, 2:], mobile[:, 1:-1, 2:]),
        (values[:, 1:-1, :-2], mobile[:, 1:-1, :-2]),
    ]
    result = jnp.zeros_like(center)
    for near_val, near_mob in pairs:
        result = result + face_mob(center_mob, near_mob) * (near_val - center)
    return result


def plain(phase_field, mobility, x_inverse, y_inverse):
    whole_inverse = lax.all_gather(y_inverse, "gy", axis=0, tiled=True)
    stacked = jnp.stack((phase_field, mobility))
    padded = extended(stacked, (("gx", 3), ("gy", 2)), 1)
    mob_near = padded[1]
    first = phase_field + step_size * laplace(padded[0], mob_near)
    first_pad = extended(first, (("gx", 2), ("gy", 1)), 1)
    second = (first + step_size * laplace(first_pad, mob_near)).astype(jnp.bfloat16)
    planes, y_rows, x_rows = second.shape
    out_rows = x_inverse.shape[0]
    segment = lax.all_gather(second, "gx", axis=2, tiled=True)
    flat = segment.reshape(planes * y_rows, segment.shape[2])
    lines = lax.dot_general(
        flat, x_inverse, (((1,), (1,)), ((), ())), preferred_element_type=jnp.float32
    )
    solved = lines.reshape(planes, y_rows, out_rows)
    chemical = solved * solved * solved - solved
    chemical_pad = extended(chemical, (("gx", 2), ("gy", 1)), 1)
    updated = (solved + step_size * laplace(chemical_pad, mob_near)).astype(jnp.bfloat16)
    columns = jnp.transpose(updated, (1, 0, 2)).reshape(y_rows, planes * x_rows)
    line_block = lax.all_to_all(columns, "gy", split_axis=1, concat_axis=0, tiled=True)
    solved_cols = jnp.dot(whole_inverse, line_block, preferred_element_type=jnp.float32)
    returned = lax.all_to_all(solved_cols, "gy", split_axis=0, concat_axis=1, tiled=True)
    return jnp.transpose(returned.reshape(y_rows, planes, x_rows), (1, 0, 2))


def half_mob(center_mob, near_mob):
    total = jnp.maximum(center_mob + near_mob, 0.25)
    inverse = pl.reciprocal(total, approx=True)
    inverse = inverse * (2.0 - total * inverse)
    return center_mob * near_mob * inverse


def sweep_plane(z, v, m, above, cols, chemical, y_rows, width, store):
    def flux_down(r, n):
        tall_v, tall_m = chemical(v[z, pl.ds(r, n + PAD), :]), m[z, pl.ds(r, n + PAD), :]
        low_v, low_m = pltpu.roll(tall_v, n + PAD - 1, 0)[:n], pltpu.roll(tall_m, n + PAD - 1, 0)[:n]
        return half_mob(tall_m[:n], low_m) * (low_v - tall_v[:n]), tall_v[:n], tall_m[:n]

    def strip(i, carried):
        r = pl.multiple_of(i * STRIP, STRIP)
        inner, mine = pl.ds(r + PAD, STRIP), pl.ds(r, STRIP)
        down, own, mob = flux_down(r + PAD, STRIP)
        stacked = jnp.concatenate([carried, down], axis=0)
        total = down - pltpu.roll(stacked, 1, 0)[PAD:]
        below = half_mob(mob, m[z + 1, inner, :]) * (chemical(v[z + 1, inner, :]) - own)
        total = total + (below - above[mine, :])
        above[mine, :] = below
        v_left, v_right, m_left, m_right = cols(z, mine)
        lane = lax.broadcasted_iota(jnp.int32, own.shape, 1)
        at_end = lane == width - 1
        v_next = jnp.where(at_end, v_right, pltpu.roll(own, width - 1, 1))
        m_next = jnp.where(at_end, m_right, pltpu.roll(mob, width - 1, 1))
        flux = half_mob(mob, m_next) * (v_next - own)
        entering = half_mob(m_left, mob[:, 0:1]) * (own[:, 0:1] - v_left)
        total = total + (flux - jnp.where(lane == 0, entering, pltpu.roll(flux, 1, 1)))
        store(mine, inner, total)
        return down[STRIP - PAD:]

    first_carry, _, _ = flux_down(0, PAD)
    lax.fori_loop(0, y_rows // STRIP, strip, first_carry)


def step_kernel(
    nx, ny, stages, w,
    phase, mobility, x_hbm, y_hbm, out, gath,
    v, m, f, second, gbuf, xsrc, xt, yinv, upd, yrecv, above, e1, r1, e2, r2,
    load_sems, row_send, row_recv, col_send, col_recv, xr_send, xr_recv,
    y_send, y_recv, gx_send, gx_recv, pair_send, pair_recv, sol_send, sol_recv,
    a2a_send, a2a_recv, ret_send, ret_recv, keep_sems, g_sems,
):
    planes, y_rows, width = phase.shape
    gx, gy = lax.axis_index("gx"), lax.axis_index("gy")
    partner = gx + 1 - 2 * lax.rem(gx, 2)
    mate = gy + 1 - 2 * lax.rem(gy, 2)
    side_half = lax.rem(gx, 2)
    half, y_half = nx // 2, ny // 2
    per = len(stages)
    chunk = planes // per
    cuts = width // w
    depth = y_rows // 2
    every = pl.ds(0, planes)

    def remote(src, dst, send, recv, x_to, y_to):
        return pltpu.make_async_remote_copy(
            src, dst, send, recv, device_id=(x_to, y_to), device_id_type=MESH)

    barrier = pltpu.get_barrier_semaphore()
    for d in range(1, ny):
        pl.semaphore_signal(barrier, inc=1, device_id=(gx, lax.rem(gy + d, ny)), device_id_type=MESH)
    for d in range(1, nx):
        pl.semaphore_signal(barrier, inc=1, device_id=(lax.rem(gx + d, nx), gy), device_id_type=MESH)

    loads = [
        pltpu.make_async_copy(phase, v.at[every, pl.ds(PAD, y_rows), :], load_sems.at[0]),
        pltpu.make_async_copy(mobility, m.at[every, pl.ds(PAD, y_rows), :], load_sems.at[1]),
        pltpu.make_async_copy(x_hbm, xsrc.at[pl.ds(0, width), :], load_sems.at[2]),
        pltpu.make_async_copy(y_hbm.at[pl.ds(0, depth), :], yinv.at[gy, 0], load_sems.at[3]),
        pltpu.make_async_copy(y_hbm.at[pl.ds(depth, depth), :], yinv.at[gy, 1], load_sems.at[4]),
    ]
    for copy in loads:
        copy.start()

    up_ok, down_ok = gy > 0, gy < ny - 1
    left_ok, right_ok = gx > 0, gx < nx - 1

    @pl.when(gy == 0)
    def _():
        for ref in (v, m, f):
            ref[every, pl.ds(0, PAD), :] = jnp.zeros((planes, PAD, width), jnp.float32)

    @pl.when(gy == ny - 1)
    def _():
        for ref in (v, m, f):
            ref[every, pl.ds(PAD + y_rows, PAD), :] = jnp.zeros((planes, PAD, width), jnp.float32)

    @pl.when(gx == 0)
    def _():
        for ref in (r1, r2):
            ref[0] = jnp.zeros(ref.shape[1:], jnp.float32)
        xsrc[pl.ds(width, 16), :] = jnp.zeros((16, xsrc.shape[1]), xsrc.dtype)

    @pl.when(gx == nx - 1)
    def _():
        for ref in (r1, r2):
            ref[1] = jnp.zeros(ref.shape[1:], jnp.float32)
        xsrc[pl.ds(width + 16, 16), :] = jnp.zeros((16, xsrc.shape[1]), xsrc.dtype)

    xsrc[pl.ds(width + 32, 96), :] = jnp.zeros((96, xsrc.shape[1]), xsrc.dtype)
    pl.semaphore_wait(barrier, ny - 1 + nx - 1)

    def edge_rows(src, lead, dst, lo, n, k, sends, recvs):
        planes_of = pl.ds(lo, n)
        down = remote(src.at[planes_of, pl.ds(lead + y_rows - PAD, PAD), :], dst.at[planes_of, pl.ds(0, PAD), :],
                      sends.at[k, 0], recvs.at[k, 0], gx, lax.rem(gy + 1, ny))
        up = remote(src.at[planes_of, pl.ds(lead, PAD), :], dst.at[planes_of, pl.ds(PAD + y_rows, PAD), :],
                    sends.at[k, 1], recvs.at[k, 1], gx, lax.rem(gy + ny - 1, ny))
        return down, up

    def columns(src, dst, k):
        right = remote(src.at[0], dst.at[0], col_send.at[k, 0], col_recv.at[k, 0], lax.rem(gx + 1, nx), gy)
        left = remote(src.at[1], dst.at[1], col_send.at[k, 1], col_recv.at[k, 1], lax.rem(gx + nx - 1, nx), gy)
        return right, left

    def inverse_rows():
        right = remote(x_hbm.at[pl.ds(width - 16, 16), :], xsrc.at[pl.ds(width, 16), :],
                       xr_send.at[0], xr_recv.at[0], lax.rem(gx + 1, nx), gy)
        left = remote(x_hbm.at[pl.ds(0, 16), :], xsrc.at[pl.ds(width + 16, 16), :],
                      xr_send.at[1], xr_recv.at[1], lax.rem(gx + nx - 1, nx), gy)
        return right, left

    def both(pair, ok_after, ok_before, act_after, act_before):
        @pl.when(ok_after)
        def _():
            act_on(pair[0], act_after)

        @pl.when(ok_before)
        def _():
            act_on(pair[1], act_before)

    def act_on(copy, act):
        if act == 0:
            copy.start()
        elif act == 1:
            copy.wait_send()
        else:
            copy.wait_recv()

    def start_rows(pair):
        both(pair, down_ok, up_ok, 0, 0)

    def sent_rows(pair):
        both(pair, down_ok, up_ok, 1, 1)

    def got_rows(pair):
        both(pair, up_ok, down_ok, 2, 2)

    def start_cols(pair):
        both(pair, right_ok, left_ok, 0, 0)

    def sent_cols(pair):
        both(pair, right_ok, left_ok, 1, 1)

    def got_cols(pair):
        both(pair, left_ok, right_ok, 2, 2)

    m_rows = edge_rows(mobility, 0, m, 0, planes, 0, row_send, row_recv)
    v_rows = edge_rows(phase, 0, v, 0, planes, 1, row_send, row_recv)
    f_rows = edge_rows(f, PAD, f, 0, planes, 2, row_send, row_recv)
    start_rows(m_rows)
    start_rows(v_rows)
    start_cols(inverse_rows())

    def y_own(d):
        return remote(y_hbm.at[pl.ds(pl.multiple_of(side_half * depth, depth), depth), :], yinv.at[gy, side_half],
                      y_send.at[0, d], y_recv.at[0, d], gx, lax.rem(gy + 2 * d, ny))

    def y_arrived(d):
        slot = lax.rem(gy - 2 * d + ny, ny)
        return remote(yinv.at[slot, side_half], yinv.at[slot, side_half], y_send.at[0, d], y_recv.at[0, d],
                      gx, lax.rem(gy + 2 * d, ny))

    def y_mate(d):
        slot = lax.rem(gy - 2 * d + ny, ny)
        src = y_hbm.at[pl.ds(pl.multiple_of(side_half * depth, depth), depth), :] if d == 0 else yinv.at[slot, side_half]
        return remote(src, yinv.at[slot, side_half], y_send.at[1, d], y_recv.at[1, d], gx, mate)

    def y_from_mate(d):
        slot = lax.rem(mate - 2 * d + ny, ny)
        return remote(yinv.at[slot, side_half], yinv.at[slot, side_half], y_send.at[1, d], y_recv.at[1, d], gx, mate)

    def y_partner(k):
        slot = lax.rem(gy + k, ny)
        return remote(yinv.at[slot, side_half], yinv.at[slot, side_half], y_send.at[2, k], y_recv.at[2, k], partner, gy)

    def y_from_partner(k):
        slot = lax.rem(gy + k, ny)
        return remote(yinv.at[slot, 1 - side_half], yinv.at[slot, 1 - side_half], y_send.at[2, k], y_recv.at[2, k],
                      partner, gy)

    for d in range(1, y_half):
        y_own(d).start()
    y_mate(0).start()

    for ref in (v, m, f):
        ref[planes] = jnp.zeros(ref.shape[1:], jnp.float32)
    above[...] = jnp.zeros_like(above)

    pack_lane = lax.broadcasted_iota(jnp.int32, (y_rows, 128), 1)
    e1[...] = jnp.zeros_like(e1)
    e2[...] = jnp.zeros_like(e2)
    loads[0].wait()
    loads[1].wait()

    @pl.loop(0, planes)
    def _(z):
        for ref, base in ((v, 0), (m, planes)):
            last = ref[z, pl.ds(PAD, y_rows), pl.ds(width - 128, 128)]
            lead = ref[z, pl.ds(PAD, y_rows), pl.ds(0, 128)]
            here = pack_lane == z + base
            e1[0] = jnp.where(here, last[:, 127:128], e1[0])
            e1[1] = jnp.where(here, lead[:, 0:1], e1[1])

    v_cols = columns(e1, r1, 0)
    f_cols = columns(e2, r2, 1)
    start_cols(v_cols)

    loads[2].wait()
    got_cols(inverse_rows())
    for b in range(nx):
        xt[b] = xsrc[:, b * width:(b + 1) * width].T

    got_rows(m_rows)
    got_rows(v_rows)
    got_cols(v_cols)

    strip_lane = lax.broadcasted_iota(jnp.int32, (STRIP, 128), 1)

    def pick(ref, side, mine, at):
        return jnp.sum(jnp.where(strip_lane == at, ref[side, mine, :], 0.0), axis=1, keepdims=True)

    def plain_value(u):
        return u

    def chemical(u):
        return u * u * u - u

    def cols_from(ref):
        def cols(z, mine):
            return (pick(ref, 0, mine, z), pick(ref, 1, mine, z),
                    pick(r1, 0, mine, z + planes), pick(r1, 1, mine, z + planes))
        return cols

    @pl.loop(0, planes)
    def _(z):
        def store(mine, inner, total):
            value = v[z, inner, :] + 2.0 * step_size * total
            f[z, inner, :] = value
            here = strip_lane == z
            e2[0, mine, :] = jnp.where(here, value[:, width - 1:width], e2[0, mine, :])
            e2[1, mine, :] = jnp.where(here, value[:, 0:1], e2[1, mine, :])

        sweep_plane(z, v, m, above, cols_from(r1), plain_value, y_rows, width, store)

    start_rows(f_rows)
    start_cols(f_cols)
    above[...] = jnp.zeros_like(above)

    def across(s, d):
        lo, n = stages[s]
        return remote(second.at[pl.ds(lo, n)], gath.at[gx, pl.ds(lo, n)], gx_send.at[s, d], gx_recv.at[s, d],
                      lax.rem(gx + 2 * d, nx), gy)

    def arrived(s, d):
        lo, n = stages[s]
        slot = lax.rem(gx - 2 * d + nx, nx)
        return remote(second.at[pl.ds(lo, n)], gath.at[slot, pl.ds(lo, n)], gx_send.at[s, d], gx_recv.at[s, d],
                      lax.rem(gx + 2 * d, nx), gy)

    def to_pair(s, d):
        lo, n = stages[s]
        slot = lax.rem(gx - 2 * d + nx, nx)
        src = second.at[pl.ds(lo, n)] if d == 0 else gath.at[slot, pl.ds(lo, n)]
        return remote(src, gath.at[slot, pl.ds(lo, n)], pair_send.at[s, d], pair_recv.at[s, d], partner, gy)

    def from_pair(s, d):
        lo, n = stages[s]
        slot = lax.rem(partner - 2 * d + nx, nx)
        return remote(second.at[pl.ds(lo, n)], gath.at[slot, pl.ds(lo, n)], pair_send.at[s, d], pair_recv.at[s, d],
                      partner, gy)

    got_rows(f_rows)
    got_cols(f_cols)

    for s in range(per):
        lo, n = stages[s]

        @pl.loop(lo, lo + n)
        def _(z):
            def store(mine, inner, total):
                second[z, mine, :] = (f[z, inner, :] + 2.0 * step_size * total).astype(second.dtype)

            sweep_plane(z, f, m, above, cols_from(r2), plain_value, y_rows, width, store)

        for d in range(1, half):
            across(s, d).start()
        to_pair(s, 0).start()

    above[...] = jnp.zeros_like(above)
    for d in range(1, y_half):
        y_arrived(d).wait_recv()
        y_mate(d).start()

    def spread(s, d):
        peer = lax.rem(gy + d, ny)
        return remote(upd.at[s, peer], yrecv.at[s, gy], a2a_send.at[s, d], a2a_recv.at[s, d], gx, peer)

    def landed(s, d):
        return remote(upd.at[s, 0], yrecv.at[s, lax.rem(gy - d + ny, ny)], a2a_send.at[s, d], a2a_recv.at[s, d],
                      gx, lax.rem(gy + d, ny))

    def back(s, d):
        peer = lax.rem(gy + d, ny)
        return remote(upd.at[s, peer], out.at[s, gy], ret_send.at[s, d], ret_recv.at[s, d], gx, peer)

    def returned(s, d):
        return remote(upd.at[s, 0], out.at[s, lax.rem(gy - d + ny, ny)], ret_send.at[s, d], ret_recv.at[s, d],
                      gx, lax.rem(gy + d, ny))

    def keep_in(s):
        return pltpu.make_async_copy(upd.at[s, gy], yrecv.at[s, gy], keep_sems.at[0, s])

    def keep_out(s):
        return pltpu.make_async_copy(upd.at[s, gy], out.at[s, gy], keep_sems.at[1, s])

    def solved_rows(s):
        lo, n = stages[s]
        return edge_rows(v, PAD, v, lo, n, s, sol_send, sol_recv)

    def fetch(z, k):
        slot = lax.rem(z, 2)
        return pltpu.make_async_copy(gath.at[lax.rem(gx + k, nx), z], gbuf.at[slot, k - 1], g_sems.at[slot, k - 1])

    def edge_cols(z, mine):
        beyond = f[z, mine, pl.ds(0, 128)]
        return (chemical(beyond[:, 15:16]), chemical(beyond[:, 16:17]),
                pick(r1, 0, mine, z + planes), pick(r1, 1, mine, z + planes))

    def solve_x(s):
        lo, n = stages[s]
        for d in range(1, half):
            arrived(s, d).wait_recv()
            to_pair(s, d).start()
        for d in range(half):
            from_pair(s, d).wait_recv()
        for k in range(1, nx):
            fetch(lo, k).start()

        @pl.loop(lo, lo + n)
        def _(z):
            @pl.when(z + 1 < lo + n)
            def _():
                for k in range(1, nx):
                    fetch(z + 1, k).start()

            total = jnp.dot(second[z], xt[gx], preferred_element_type=jnp.float32)
            for k in range(1, nx):
                fetch(z, k).wait()
                total = total + jnp.dot(
                    gbuf[lax.rem(z, 2), k - 1], xt[lax.rem(gx + k, nx)], preferred_element_type=jnp.float32)
            v[z, pl.ds(PAD, y_rows), :] = total[:, :width]
            f[z, pl.ds(0, y_rows), pl.ds(0, 128)] = total[:, width:]

        start_rows(solved_rows(s))
        got_rows(solved_rows(s))

        @pl.loop(s * chunk, (s + 1) * chunk)
        def _(z):
            def store(mine, inner, total):
                value = (v[z, inner, :] + 2.0 * step_size * total).astype(upd.dtype)
                for c in range(cuts):
                    upd[s, (z - s * chunk) * cuts + c, mine, :] = value[:, c * w:(c + 1) * w]

            sweep_plane(z, v, m, above, edge_cols, chemical, y_rows, width, store)

        keep_in(s).start()

        @pl.loop(1, ny)
        def _(d):
            spread(s, d).start()

    def share_inverse():
        for d in range(y_half):
            y_from_mate(d).wait_recv()
        for k in range(1, ny):
            y_partner(k).start()

    def solve_y(s):
        if s == 0:
            loads[3].wait()
            loads[4].wait()
            for k in range(1, ny):
                y_from_partner(k).wait_recv()
        keep_in(s).wait()

        @pl.loop(1, ny)
        def _(d):
            landed(s, d).wait_recv()
            spread(s, d).wait_send()

        def block(d):
            peer = lax.rem(gy + d, ny)
            lines = yrecv[s].reshape(ny * y_rows, w)
            upd[s, peer] = jnp.dot(
                yinv[peer].reshape(y_rows, ny * y_rows), lines, preferred_element_type=jnp.float32).astype(upd.dtype)

        @pl.loop(1, ny)
        def _(d):
            block(d)
            back(s, d).start()

        block(0)
        keep_out(s).start()

    sent_rows(f_rows)
    for s in range(per):
        solve_x(s)
        if s == 0:
            share_inverse()
        else:
            solve_y(s - 1)
    solve_y(per - 1)

    for pair in (m_rows, v_rows):
        sent_rows(pair)
    for pair in (v_cols, f_cols, inverse_rows()):
        sent_cols(pair)
    for d in range(1, y_half):
        y_own(d).wait_send()
    for d in range(y_half):
        y_mate(d).wait_send()
    for k in range(1, ny):
        y_partner(k).wait_send()
    for s in range(per):
        for d in range(1, half):
            across(s, d).wait_send()
        for d in range(half):
            to_pair(s, d).wait_send()
        sent_rows(solved_rows(s))
        keep_out(s).wait()

        @pl.loop(1, ny)
        def _(d):
            back(s, d).wait_send()
            returned(s, d).wait_recv()


def local(per, phase_field, mobility, x_inverse, y_inverse):
    planes, y_rows, width = phase_field.shape
    nx, ny = lax.axis_size("gx"), lax.axis_size("gy")
    chunk = planes // per
    w = chunk * width // ny
    ends = [min((s + 1) * chunk + 1, planes) for s in range(per)]
    starts = [0] + ends[:-1]
    stages = [(lo, hi - lo) for lo, hi in zip(starts, ends)]
    f32, bf16, dma = jnp.float32, jnp.bfloat16, pltpu.SemaphoreType.DMA
    tall = pltpu.VMEM((planes + 1, y_rows + 2 * PAD, width), f32)
    edges = pltpu.VMEM((2, y_rows, 128), f32)
    any_spec = pl.BlockSpec(memory_space=pl.ANY)
    lines, _ = pl.pallas_call(
        functools.partial(step_kernel, nx, ny, stages, w),
        out_shape=(
            jax.ShapeDtypeStruct((per, ny, y_rows, w), bf16),
            jax.ShapeDtypeStruct((nx, planes, y_rows, width), bf16),
        ),
        in_specs=[any_spec] * 4,
        out_specs=(any_spec, any_spec),
        scratch_shapes=[
            tall, tall, tall,
            pltpu.VMEM((planes, y_rows, width), bf16),
            pltpu.VMEM((2, nx - 1, y_rows, width), bf16),
            pltpu.VMEM((width + 128, nx * width), bf16),
            pltpu.VMEM((nx, width, width + 128), bf16),
            pltpu.VMEM((ny, 2, y_rows // 2, ny * y_rows), bf16),
            pltpu.VMEM((per, ny, y_rows, w), bf16),
            pltpu.VMEM((per, ny, y_rows, w), bf16),
            pltpu.VMEM((y_rows, width), f32),
            edges, edges, edges, edges,
            dma((5,)), dma((3, 2)), dma((3, 2)), dma((2, 2)), dma((2, 2)), dma((2,)), dma((2,)),
            dma((3, ny)), dma((3, ny)),
            dma((per, nx // 2)), dma((per, nx // 2)), dma((per, nx // 2)), dma((per, nx // 2)),
            dma((per, 2)), dma((per, 2)),
            dma((per, ny)), dma((per, ny)), dma((per, ny)), dma((per, ny)),
            dma((2, per)), dma((2, nx - 1)),
        ],
        compiler_params=pltpu.CompilerParams(
            collective_id=0, has_side_effects=True, vmem_limit_bytes=62 * 2**20),
        cost_estimate=pl.CostEstimate(
            flops=8400 * phase_field.size, bytes_accessed=40 * phase_field.size, transcendentals=0),
    )(phase_field, mobility, x_inverse, y_inverse)
    lines = lines.reshape(planes, width // w, y_rows, w)
    return jnp.transpose(lines, (0, 2, 1, 3)).reshape(planes, y_rows, width).astype(jnp.float32)


def chunks(planes, y_rows, width, nx, ny):
    if nx % 2 or ny % 2 or nx < 4 or ny < 4 or y_rows % STRIP or width % 128 or planes > 64:
        return 0
    if 30 * planes * y_rows * width > 64 * 2**20:
        return 0
    for per in (4, 2, 1):
        if planes % per == 0 and planes // per * width % ny == 0:
            w = planes // per * width // ny
            if w % 128 == 0 and width % w == 0:
                return per
    return 0


def solution(mesh):
    placed = (P(None, "gy", "gx"), P(None, "gy", "gx"), P("gx", None), P("gy", None))
    nx, ny = mesh.shape["gx"], mesh.shape["gy"]

    def step(phase_field, mobility, x_inverse, y_inverse):
        planes, rows, cols = phase_field.shape
        per = chunks(planes, rows // ny, cols // nx, nx, ny)
        body = functools.partial(local, per) if per else plain
        return jax.shard_map(
            body, mesh=mesh, in_specs=placed, out_specs=P(None, "gy", "gx"), check_vma=False
        )(phase_field, mobility, x_inverse, y_inverse)

    return step
```

```python
import functools

import jax
import jax.numpy as jnp
from jax import lax
from jax.experimental import pallas as pl
from jax.experimental.pallas import tpu as pltpu
from jax.sharding import PartitionSpec as P

step_size = 0.15
PAD = 8
STRIP = 32
MESH = pl.DeviceIdType.MESH


def face_mob(center_mob, near_mob):
    return 2.0 * center_mob * near_mob / jnp.maximum(center_mob + near_mob, 0.25)


def extended(x, sides, width):
    for axis, dim in sides:
        size, length = (lax.axis_size(axis), x.shape[dim])
        up = [(i, (i + 1) % size) for i in range(size - 1)]
        down = [(j, i) for i, j in up]
        last = lax.slice_in_dim(x, length - width, length, axis=dim)
        leading = lax.slice_in_dim(x, 0, width, axis=dim)
        before = lax.ppermute(last, axis, up)
        after = lax.ppermute(leading, axis, down)
        x = jnp.concatenate([before, x, after], axis=dim)
    return x


def laplace(values, mobile):
    values_z = jnp.pad(values, ((1, 1), (0, 0), (0, 0)))
    mobile_z = jnp.pad(mobile, ((1, 1), (0, 0), (0, 0)))
    center = values[:, 1:-1, 1:-1]
    center_mob = mobile[:, 1:-1, 1:-1]
    pairs = [
        (values_z[2:, 1:-1, 1:-1], mobile_z[2:, 1:-1, 1:-1]),
        (values_z[:-2, 1:-1, 1:-1], mobile_z[:-2, 1:-1, 1:-1]),
        (values[:, 2:, 1:-1], mobile[:, 2:, 1:-1]),
        (values[:, :-2, 1:-1], mobile[:, :-2, 1:-1]),
        (values[:, 1:-1, 2:], mobile[:, 1:-1, 2:]),
        (values[:, 1:-1, :-2], mobile[:, 1:-1, :-2]),
    ]
    result = jnp.zeros_like(center)
    for near_val, near_mob in pairs:
        result = result + face_mob(center_mob, near_mob) * (near_val - center)
    return result


def plain(phase_field, mobility, x_inverse, y_inverse):
    whole_inverse = lax.all_gather(y_inverse, "gy", axis=0, tiled=True)
    stacked = jnp.stack((phase_field, mobility))
    padded = extended(stacked, (("gx", 3), ("gy", 2)), 1)
    mob_near = padded[1]
    first = phase_field + step_size * laplace(padded[0], mob_near)
    first_pad = extended(first, (("gx", 2), ("gy", 1)), 1)
    second = (first + step_size * laplace(first_pad, mob_near)).astype(jnp.bfloat16)
    planes, y_rows, x_rows = second.shape
    out_rows = x_inverse.shape[0]
    segment = lax.all_gather(second, "gx", axis=2, tiled=True)
    flat = segment.reshape(planes * y_rows, segment.shape[2])
    lines = lax.dot_general(
        flat, x_inverse, (((1,), (1,)), ((), ())), preferred_element_type=jnp.float32
    )
    solved = lines.reshape(planes, y_rows, out_rows)
    chemical = solved * solved * solved - solved
    chemical_pad = extended(chemical, (("gx", 2), ("gy", 1)), 1)
    updated = (solved + step_size * laplace(chemical_pad, mob_near)).astype(jnp.bfloat16)
    columns = jnp.transpose(updated, (1, 0, 2)).reshape(y_rows, planes * x_rows)
    line_block = lax.all_to_all(columns, "gy", split_axis=1, concat_axis=0, tiled=True)
    solved_cols = jnp.dot(whole_inverse, line_block, preferred_element_type=jnp.float32)
    returned = lax.all_to_all(solved_cols, "gy", split_axis=0, concat_axis=1, tiled=True)
    return jnp.transpose(returned.reshape(y_rows, planes, x_rows), (1, 0, 2))


def half_mob(center_mob, near_mob):
    total = jnp.maximum(center_mob + near_mob, 0.25)
    inverse = pl.reciprocal(total, approx=True)
    inverse = inverse * (2.0 - total * inverse)
    return center_mob * near_mob * inverse


def sweep_plane(z, v, m, above, cols, chemical, y_rows, width, store):
    def flux_down(r, n):
        tall_v, tall_m = chemical(v[z, pl.ds(r, n + PAD), :]), m[z, pl.ds(r, n + PAD), :]
        low_v, low_m = pltpu.roll(tall_v, n + PAD - 1, 0)[:n], pltpu.roll(tall_m, n + PAD - 1, 0)[:n]
        return half_mob(tall_m[:n], low_m) * (low_v - tall_v[:n]), tall_v[:n], tall_m[:n]

    def strip(i, carried):
        r = pl.multiple_of(i * STRIP, STRIP)
        inner, mine = pl.ds(r + PAD, STRIP), pl.ds(r, STRIP)
        down, own, mob = flux_down(r + PAD, STRIP)
        stacked = jnp.concatenate([carried, down], axis=0)
        total = down - pltpu.roll(stacked, 1, 0)[PAD:]
        below = half_mob(mob, m[z + 1, inner, :]) * (chemical(v[z + 1, inner, :]) - own)
        total = total + (below - above[mine, :])
        above[mine, :] = below
        v_left, v_right, m_left, m_right = cols(z, mine)
        lane = lax.broadcasted_iota(jnp.int32, own.shape, 1)
        at_end = lane == width - 1
        v_next = jnp.where(at_end, v_right, pltpu.roll(own, width - 1, 1))
        m_next = jnp.where(at_end, m_right, pltpu.roll(mob, width - 1, 1))
        flux = half_mob(mob, m_next) * (v_next - own)
        entering = half_mob(m_left, mob[:, 0:1]) * (own[:, 0:1] - v_left)
        total = total + (flux - jnp.where(lane == 0, entering, pltpu.roll(flux, 1, 1)))
        store(mine, inner, total)
        return down[STRIP - PAD:]

    first_carry, _, _ = flux_down(0, PAD)
    lax.fori_loop(0, y_rows // STRIP, strip, first_carry)


def step_kernel(
    nx, ny, stages, w,
    phase, mobility, x_hbm, y_hbm, out, gath,
    v, m, f, second, gbuf, xsrc, xt, yinv, upd, yrecv, above1, above2, above3, e1, r1, e2, r2,
    load_sems, in_sems, row_send, row_recv, f_send, f_recv, col_send, col_recv, xr_send, xr_recv,
    y_send, y_recv, gx_send, gx_recv, pair_send, pair_recv, sol_send, sol_recv,
    a2a_send, a2a_recv, ret_send, ret_recv, keep_sems, g_sems,
):
    planes, y_rows, width = phase.shape
    gx, gy = lax.axis_index("gx"), lax.axis_index("gy")
    partner = gx + 1 - 2 * lax.rem(gx, 2)
    mate = gy + 1 - 2 * lax.rem(gy, 2)
    side_half = lax.rem(gx, 2)
    half, y_half = nx // 2, ny // 2
    per = len(stages)
    chunk = planes // per
    cuts = width // w
    depth = y_rows // 2
    every = pl.ds(0, planes)

    def remote(src, dst, send, recv, x_to, y_to):
        return pltpu.make_async_remote_copy(
            src, dst, send, recv, device_id=(x_to, y_to), device_id_type=MESH)

    barrier = pltpu.get_barrier_semaphore()
    for d in range(1, ny):
        pl.semaphore_signal(barrier, inc=1, device_id=(gx, lax.rem(gy + d, ny)), device_id_type=MESH)
    for d in range(1, nx):
        pl.semaphore_signal(barrier, inc=1, device_id=(lax.rem(gx + d, nx), gy), device_id_type=MESH)

    loads = [
        pltpu.make_async_copy(x_hbm, xsrc.at[pl.ds(0, width), :], load_sems.at[0]),
        pltpu.make_async_copy(y_hbm.at[pl.ds(0, depth), :], yinv.at[gy, 0], load_sems.at[1]),
        pltpu.make_async_copy(y_hbm.at[pl.ds(depth, depth), :], yinv.at[gy, 1], load_sems.at[2]),
    ]
    def load(g):
        group = pl.ds(g * chunk, chunk)
        return (pltpu.make_async_copy(phase.at[group], v.at[group, pl.ds(PAD, y_rows), :], in_sems.at[g, 0]),
                pltpu.make_async_copy(mobility.at[group], m.at[group, pl.ds(PAD, y_rows), :], in_sems.at[g, 1]))

    for g in range(per):
        for copy in load(g):
            copy.start()
    for copy in loads:
        copy.start()

    up_ok, down_ok = gy > 0, gy < ny - 1
    left_ok, right_ok = gx > 0, gx < nx - 1

    @pl.when(gy == 0)
    def _():
        for ref in (v, m, f):
            ref[every, pl.ds(0, PAD), :] = jnp.zeros((planes, PAD, width), jnp.float32)

    @pl.when(gy == ny - 1)
    def _():
        for ref in (v, m, f):
            ref[every, pl.ds(PAD + y_rows, PAD), :] = jnp.zeros((planes, PAD, width), jnp.float32)

    @pl.when(gx == 0)
    def _():
        r1[0] = jnp.zeros(r1.shape[1:], jnp.float32)
        for g in range(per):
            r2[g, 0] = jnp.zeros(r1.shape[1:], jnp.float32)
        xsrc[pl.ds(width, 16), :] = jnp.zeros((16, xsrc.shape[1]), xsrc.dtype)

    @pl.when(gx == nx - 1)
    def _():
        r1[1] = jnp.zeros(r1.shape[1:], jnp.float32)
        for g in range(per):
            r2[g, 1] = jnp.zeros(r1.shape[1:], jnp.float32)
        xsrc[pl.ds(width + 16, 16), :] = jnp.zeros((16, xsrc.shape[1]), xsrc.dtype)

    xsrc[pl.ds(width + 32, 96), :] = jnp.zeros((96, xsrc.shape[1]), xsrc.dtype)
    pl.semaphore_wait(barrier, ny - 1 + nx - 1)

    def edge_rows(src, lead, dst, lo, n, k, sends, recvs):
        planes_of = pl.ds(lo, n)
        down = remote(src.at[planes_of, pl.ds(lead + y_rows - PAD, PAD), :], dst.at[planes_of, pl.ds(0, PAD), :],
                      sends.at[k, 0], recvs.at[k, 0], gx, lax.rem(gy + 1, ny))
        up = remote(src.at[planes_of, pl.ds(lead, PAD), :], dst.at[planes_of, pl.ds(PAD + y_rows, PAD), :],
                    sends.at[k, 1], recvs.at[k, 1], gx, lax.rem(gy + ny - 1, ny))
        return down, up

    def columns(src, dst, k):
        right = remote(src.at[0], dst.at[0], col_send.at[k, 0], col_recv.at[k, 0], lax.rem(gx + 1, nx), gy)
        left = remote(src.at[1], dst.at[1], col_send.at[k, 1], col_recv.at[k, 1], lax.rem(gx + nx - 1, nx), gy)
        return right, left

    def inverse_rows():
        right = remote(x_hbm.at[pl.ds(width - 16, 16), :], xsrc.at[pl.ds(width, 16), :],
                       xr_send.at[0], xr_recv.at[0], lax.rem(gx + 1, nx), gy)
        left = remote(x_hbm.at[pl.ds(0, 16), :], xsrc.at[pl.ds(width + 16, 16), :],
                      xr_send.at[1], xr_recv.at[1], lax.rem(gx + nx - 1, nx), gy)
        return right, left

    def both(pair, ok_after, ok_before, act_after, act_before):
        @pl.when(ok_after)
        def _():
            act_on(pair[0], act_after)

        @pl.when(ok_before)
        def _():
            act_on(pair[1], act_before)

    def act_on(copy, act):
        if act == 0:
            copy.start()
        elif act == 1:
            copy.wait_send()
        else:
            copy.wait_recv()

    def start_rows(pair):
        both(pair, down_ok, up_ok, 0, 0)

    def sent_rows(pair):
        both(pair, down_ok, up_ok, 1, 1)

    def got_rows(pair):
        both(pair, up_ok, down_ok, 2, 2)

    def start_cols(pair):
        both(pair, right_ok, left_ok, 0, 0)

    def sent_cols(pair):
        both(pair, right_ok, left_ok, 1, 1)

    def got_cols(pair):
        both(pair, left_ok, right_ok, 2, 2)

    m_rows = edge_rows(mobility, 0, m, 0, planes, 0, row_send, row_recv)
    v_rows = edge_rows(phase, 0, v, 0, planes, 1, row_send, row_recv)
    start_rows(m_rows)
    start_rows(v_rows)
    start_cols(inverse_rows())

    def y_own(d):
        return remote(y_hbm.at[pl.ds(pl.multiple_of(side_half * depth, depth), depth), :], yinv.at[gy, side_half],
                      y_send.at[0, d], y_recv.at[0, d], gx, lax.rem(gy + 2 * d, ny))

    def y_arrived(d):
        slot = lax.rem(gy - 2 * d + ny, ny)
        return remote(yinv.at[slot, side_half], yinv.at[slot, side_half], y_send.at[0, d], y_recv.at[0, d],
                      gx, lax.rem(gy + 2 * d, ny))

    def y_mate(d):
        slot = lax.rem(gy - 2 * d + ny, ny)
        src = y_hbm.at[pl.ds(pl.multiple_of(side_half * depth, depth), depth), :] if d == 0 else yinv.at[slot, side_half]
        return remote(src, yinv.at[slot, side_half], y_send.at[1, d], y_recv.at[1, d], gx, mate)

    def y_from_mate(d):
        slot = lax.rem(mate - 2 * d + ny, ny)
        return remote(yinv.at[slot, side_half], yinv.at[slot, side_half], y_send.at[1, d], y_recv.at[1, d], gx, mate)

    def y_partner(k):
        slot = lax.rem(gy + k, ny)
        return remote(yinv.at[slot, side_half], yinv.at[slot, side_half], y_send.at[2, k], y_recv.at[2, k], partner, gy)

    def y_from_partner(k):
        slot = lax.rem(gy + k, ny)
        return remote(yinv.at[slot, 1 - side_half], yinv.at[slot, 1 - side_half], y_send.at[2, k], y_recv.at[2, k],
                      partner, gy)

    for ref in (v, m, f):
        ref[planes] = jnp.zeros(ref.shape[1:], jnp.float32)
    for ref in (above1, above2, above3):
        ref[...] = jnp.zeros_like(ref)

    pack_lane = lax.broadcasted_iota(jnp.int32, (y_rows, 128), 1)
    e1[...] = jnp.zeros_like(e1)
    e2[...] = jnp.zeros_like(e2)
    for g in range(per):
        for copy in load(g):
            copy.wait()

        @pl.loop(g * chunk, (g + 1) * chunk)
        def _(z):
            for ref, base in ((v, 0), (m, planes)):
                last = ref[z, pl.ds(PAD, y_rows), pl.ds(width - 128, 128)]
                lead = ref[z, pl.ds(PAD, y_rows), pl.ds(0, 128)]
                here = pack_lane == z + base
                e1[0] = jnp.where(here, last[:, 127:128], e1[0])
                e1[1] = jnp.where(here, lead[:, 0:1], e1[1])

    v_cols = columns(e1, r1, 0)
    start_cols(v_cols)

    loads[0].wait()
    got_cols(inverse_rows())
    for b in range(nx):
        xt[b] = xsrc[:, b * width:(b + 1) * width].T

    got_rows(m_rows)
    got_rows(v_rows)
    got_cols(v_cols)
    for d in range(1, y_half):
        y_own(d).start()
    y_mate(0).start()

    strip_lane = lax.broadcasted_iota(jnp.int32, (STRIP, 128), 1)

    def pick(ref, side, mine, at):
        return jnp.sum(jnp.where(strip_lane == at, ref[side, mine, :], 0.0), axis=1, keepdims=True)

    def plain_value(u):
        return u

    def chemical(u):
        return u * u * u - u

    def cols_from(ref):
        def cols(z, mine):
            return (pick(ref, 0, mine, z), pick(ref, 1, mine, z),
                    pick(r1, 0, mine, z + planes), pick(r1, 1, mine, z + planes))
        return cols

    def f_rows(s):
        lo, n = stages[s]
        return edge_rows(f, PAD, f, lo, n, s, f_send, f_recv)

    def f_cols(s):
        return columns(e2.at[s], r2.at[s], 1 + s)

    def make_first(s):
        lo, n = stages[s]
        beyond = lo + n

        @pl.loop(lo + (1 if s else 0), min(beyond + 1, planes))
        def _(z):
            def store(mine, inner, total):
                value = v[z, inner, :] + 2.0 * step_size * total
                f[z, inner, :] = value
                here = strip_lane == z
                t = s if beyond == planes else s + lax.div(z, beyond)
                e2[t, 0, mine, :] = jnp.where(here, value[:, width - 1:width], e2[t, 0, mine, :])
                e2[t, 1, mine, :] = jnp.where(here, value[:, 0:1], e2[t, 1, mine, :])

            sweep_plane(z, v, m, above1, cols_from(r1), plain_value, y_rows, width, store)

        start_rows(f_rows(s))
        start_cols(f_cols(s))

    def make_second(s):
        lo, n = stages[s]
        got_rows(f_rows(s))
        got_cols(f_cols(s))

        @pl.loop(lo, lo + n)
        def _(z):
            def store(mine, inner, total):
                second[z, mine, :] = (f[z, inner, :] + 2.0 * step_size * total).astype(second.dtype)

            sweep_plane(z, f, m, above2, cols_from(r2.at[s]), plain_value, y_rows, width, store)

    def across(s, d):
        lo, n = stages[s]
        return remote(second.at[pl.ds(lo, n)], gath.at[gx, pl.ds(lo, n)], gx_send.at[s, d], gx_recv.at[s, d],
                      lax.rem(gx + 2 * d, nx), gy)

    def arrived(s, d):
        lo, n = stages[s]
        slot = lax.rem(gx - 2 * d + nx, nx)
        return remote(second.at[pl.ds(lo, n)], gath.at[slot, pl.ds(lo, n)], gx_send.at[s, d], gx_recv.at[s, d],
                      lax.rem(gx + 2 * d, nx), gy)

    def to_pair(s, d):
        lo, n = stages[s]
        slot = lax.rem(gx - 2 * d + nx, nx)
        src = second.at[pl.ds(lo, n)] if d == 0 else gath.at[slot, pl.ds(lo, n)]
        return remote(src, gath.at[slot, pl.ds(lo, n)], pair_send.at[s, d], pair_recv.at[s, d], partner, gy)

    def from_pair(s, d):
        lo, n = stages[s]
        slot = lax.rem(partner - 2 * d + nx, nx)
        return remote(second.at[pl.ds(lo, n)], gath.at[slot, pl.ds(lo, n)], pair_send.at[s, d], pair_recv.at[s, d],
                      partner, gy)

    def send_second(s):
        for d in range(1, half):
            across(s, d).start()
        to_pair(s, 0).start()

    def home(s, owner):
        off = pl.multiple_of(lax.rem(owner, cuts) * w, w)
        return out.at[s * chunk + lax.div(owner, cuts), :, pl.ds(off, w)]

    def spread(s, d):
        peer = lax.rem(gy + d, ny)
        return remote(upd.at[s, peer], yrecv.at[s, gy], a2a_send.at[s, d], a2a_recv.at[s, d], gx, peer)

    def landed(s, d):
        return remote(upd.at[s, 0], yrecv.at[s, lax.rem(gy - d + ny, ny)], a2a_send.at[s, d], a2a_recv.at[s, d],
                      gx, lax.rem(gy + d, ny))

    def back(s, d):
        peer = lax.rem(gy + d, ny)
        return remote(upd.at[s, peer], home(s, gy), ret_send.at[s, d], ret_recv.at[s, d], gx, peer)

    def returned(s, d):
        return remote(upd.at[s, 0], home(s, lax.rem(gy - d + ny, ny)), ret_send.at[s, d], ret_recv.at[s, d],
                      gx, lax.rem(gy + d, ny))

    def keep_in(s):
        return pltpu.make_async_copy(upd.at[s, gy], yrecv.at[s, gy], keep_sems.at[0, s])

    def keep_out(s):
        return pltpu.make_async_copy(upd.at[s, gy], home(s, gy), keep_sems.at[1, s])

    def solved_rows(s):
        lo, n = stages[s]
        return edge_rows(v, PAD, v, lo, n, s, sol_send, sol_recv)

    def fetch(z, k):
        slot = lax.rem(z, 2)
        return pltpu.make_async_copy(gath.at[lax.rem(gx + k, nx), z], gbuf.at[slot, k - 1], g_sems.at[slot, k - 1])

    def edge_cols(z, mine):
        beyond = f[z, mine, pl.ds(0, 128)]
        return (chemical(beyond[:, 15:16]), chemical(beyond[:, 16:17]),
                pick(r1, 0, mine, z + planes), pick(r1, 1, mine, z + planes))

    def solve_x(s):
        lo, n = stages[s]
        for d in range(1, half):
            arrived(s, d).wait_recv()
            to_pair(s, d).start()
        if s + 1 < per:
            send_second(s + 1)
        if s == 0:
            for d in range(1, y_half):
                y_arrived(d).wait_recv()
                y_mate(d).start()
        sent_rows(f_rows(s))
        for d in range(half):
            from_pair(s, d).wait_recv()
        for k in range(1, nx):
            fetch(lo, k).start()

        @pl.loop(lo, lo + n)
        def _(z):
            @pl.when(z + 1 < lo + n)
            def _():
                for k in range(1, nx):
                    fetch(z + 1, k).start()

            total = jnp.dot(second[z], xt[gx], preferred_element_type=jnp.float32)
            for k in range(1, nx):
                fetch(z, k).wait()
                total = total + jnp.dot(
                    gbuf[lax.rem(z, 2), k - 1], xt[lax.rem(gx + k, nx)], preferred_element_type=jnp.float32)
            v[z, pl.ds(PAD, y_rows), :] = total[:, :width]
            f[z, pl.ds(0, y_rows), pl.ds(0, 128)] = total[:, width:]

        start_rows(solved_rows(s))
        got_rows(solved_rows(s))

        @pl.loop(s * chunk, (s + 1) * chunk)
        def _(z):
            def store(mine, inner, total):
                value = (v[z, inner, :] + 2.0 * step_size * total).astype(upd.dtype)
                for c in range(cuts):
                    upd[s, (z - s * chunk) * cuts + c, mine, :] = value[:, c * w:(c + 1) * w]

            sweep_plane(z, v, m, above3, edge_cols, chemical, y_rows, width, store)

        keep_in(s).start()

        @pl.loop(1, ny)
        def _(d):
            spread(s, d).start()

    def share_inverse():
        for d in range(y_half):
            y_from_mate(d).wait_recv()
        for k in range(1, ny):
            y_partner(k).start()

    def solve_y(s):
        if s == 0:
            loads[1].wait()
            loads[2].wait()
            for k in range(1, ny):
                y_from_partner(k).wait_recv()
        keep_in(s).wait()

        @pl.loop(1, ny)
        def _(d):
            landed(s, d).wait_recv()
            spread(s, d).wait_send()

        def block(d):
            peer = lax.rem(gy + d, ny)
            lines = yrecv[s].reshape(ny * y_rows, w)
            upd[s, peer] = jnp.dot(
                yinv[peer].reshape(y_rows, ny * y_rows), lines, preferred_element_type=jnp.float32).astype(upd.dtype)

        @pl.loop(1, ny)
        def _(d):
            block(d)
            back(s, d).start()

        block(0)
        keep_out(s).start()

    make_first(0)
    make_second(0)
    send_second(0)
    for s in range(per):
        if s + 1 < per:
            make_first(s + 1)
            make_second(s + 1)
        solve_x(s)
        if s == 1:
            share_inverse()
        if s > 0:
            solve_y(s - 1)
    solve_y(per - 1)

    for pair in (m_rows, v_rows):
        sent_rows(pair)
    for pair in [v_cols, inverse_rows()] + [f_cols(s) for s in range(per)]:
        sent_cols(pair)
    for d in range(1, y_half):
        y_own(d).wait_send()
    for d in range(y_half):
        y_mate(d).wait_send()
    for k in range(1, ny):
        y_partner(k).wait_send()
    for s in range(per):
        for d in range(1, half):
            across(s, d).wait_send()
        for d in range(half):
            to_pair(s, d).wait_send()
        sent_rows(solved_rows(s))
        keep_out(s).wait()

        @pl.loop(1, ny)
        def _(d):
            back(s, d).wait_send()
            returned(s, d).wait_recv()


def local(per, phase_field, mobility, x_inverse, y_inverse):
    planes, y_rows, width = phase_field.shape
    nx, ny = lax.axis_size("gx"), lax.axis_size("gy")
    chunk = planes // per
    w = chunk * width // ny
    ends = [min((s + 1) * chunk + 1, planes) for s in range(per)]
    starts = [0] + ends[:-1]
    stages = [(lo, hi - lo) for lo, hi in zip(starts, ends)]
    f32, bf16, dma = jnp.float32, jnp.bfloat16, pltpu.SemaphoreType.DMA
    tall = pltpu.VMEM((planes + 1, y_rows + 2 * PAD, width), f32)
    edges = pltpu.VMEM((2, y_rows, 128), f32)
    staged_edges = pltpu.VMEM((per, 2, y_rows, 128), f32)
    above = pltpu.VMEM((y_rows, width), f32)
    any_spec = pl.BlockSpec(memory_space=pl.ANY)
    lines, _ = pl.pallas_call(
        functools.partial(step_kernel, nx, ny, stages, w),
        out_shape=(
            jax.ShapeDtypeStruct((planes, y_rows, width), bf16),
            jax.ShapeDtypeStruct((nx, planes, y_rows, width), bf16),
        ),
        in_specs=[any_spec] * 4,
        out_specs=(any_spec, any_spec),
        scratch_shapes=[
            tall, tall, tall,
            pltpu.VMEM((planes, y_rows, width), bf16),
            pltpu.VMEM((2, nx - 1, y_rows, width), bf16),
            pltpu.VMEM((width + 128, nx * width), bf16),
            pltpu.VMEM((nx, width, width + 128), bf16),
            pltpu.VMEM((ny, 2, y_rows // 2, ny * y_rows), bf16),
            pltpu.VMEM((per, ny, y_rows, w), bf16),
            pltpu.VMEM((per, ny, y_rows, w), bf16),
            above, above, above,
            edges, edges, staged_edges, staged_edges,
            dma((3,)), dma((per, 2)), dma((2, 2)), dma((2, 2)), dma((per, 2)), dma((per, 2)),
            dma((1 + per, 2)), dma((1 + per, 2)), dma((2,)), dma((2,)),
            dma((3, ny)), dma((3, ny)),
            dma((per, nx // 2)), dma((per, nx // 2)), dma((per, nx // 2)), dma((per, nx // 2)),
            dma((per, 2)), dma((per, 2)),
            dma((per, ny)), dma((per, ny)), dma((per, ny)), dma((per, ny)),
            dma((2, per)), dma((2, nx - 1)),
        ],
        compiler_params=pltpu.CompilerParams(
            collective_id=0, has_side_effects=True, vmem_limit_bytes=62 * 2**20),
        cost_estimate=pl.CostEstimate(
            flops=8400 * phase_field.size, bytes_accessed=40 * phase_field.size, transcendentals=0),
    )(phase_field, mobility, x_inverse, y_inverse)
    return lines.astype(jnp.float32)


def chunks(planes, y_rows, width, nx, ny):
    if nx % 2 or ny % 2 or nx < 4 or ny < 4 or y_rows % STRIP or width % 128 or planes > 64:
        return 0
    if 30 * planes * y_rows * width > 64 * 2**20:
        return 0
    for per in (4, 2):
        if planes % per == 0 and planes // per * width % ny == 0:
            w = planes // per * width // ny
            if w % 128 == 0 and width % w == 0:
                return per
    return 0


def solution(mesh):
    placed = (P(None, "gy", "gx"), P(None, "gy", "gx"), P("gx", None), P("gy", None))
    nx, ny = mesh.shape["gx"], mesh.shape["gy"]

    def step(phase_field, mobility, x_inverse, y_inverse):
        planes, rows, cols = phase_field.shape
        per = chunks(planes, rows // ny, cols // nx, nx, ny)
        body = functools.partial(local, per) if per else plain
        return jax.shard_map(
            body, mesh=mesh, in_specs=placed, out_specs=P(None, "gy", "gx"), check_vma=False
        )(phase_field, mobility, x_inverse, y_inverse)

    return step
```

```python
import functools

import jax
import jax.numpy as jnp
from jax import lax
from jax.experimental import pallas as pl
from jax.experimental.pallas import tpu as pltpu
from jax.sharding import PartitionSpec as P

step_size = 0.15
PAD = 8
STRIP = 32
MESH = pl.DeviceIdType.MESH


def face_mob(center_mob, near_mob):
    return 2.0 * center_mob * near_mob / jnp.maximum(center_mob + near_mob, 0.25)


def extended(x, sides, width):
    for axis, dim in sides:
        size, length = (lax.axis_size(axis), x.shape[dim])
        up = [(i, (i + 1) % size) for i in range(size - 1)]
        down = [(j, i) for i, j in up]
        last = lax.slice_in_dim(x, length - width, length, axis=dim)
        leading = lax.slice_in_dim(x, 0, width, axis=dim)
        before = lax.ppermute(last, axis, up)
        after = lax.ppermute(leading, axis, down)
        x = jnp.concatenate([before, x, after], axis=dim)
    return x


def laplace(values, mobile):
    values_z = jnp.pad(values, ((1, 1), (0, 0), (0, 0)))
    mobile_z = jnp.pad(mobile, ((1, 1), (0, 0), (0, 0)))
    center = values[:, 1:-1, 1:-1]
    center_mob = mobile[:, 1:-1, 1:-1]
    pairs = [
        (values_z[2:, 1:-1, 1:-1], mobile_z[2:, 1:-1, 1:-1]),
        (values_z[:-2, 1:-1, 1:-1], mobile_z[:-2, 1:-1, 1:-1]),
        (values[:, 2:, 1:-1], mobile[:, 2:, 1:-1]),
        (values[:, :-2, 1:-1], mobile[:, :-2, 1:-1]),
        (values[:, 1:-1, 2:], mobile[:, 1:-1, 2:]),
        (values[:, 1:-1, :-2], mobile[:, 1:-1, :-2]),
    ]
    result = jnp.zeros_like(center)
    for near_val, near_mob in pairs:
        result = result + face_mob(center_mob, near_mob) * (near_val - center)
    return result


def plain(phase_field, mobility, x_inverse, y_inverse):
    whole_inverse = lax.all_gather(y_inverse, "gy", axis=0, tiled=True)
    stacked = jnp.stack((phase_field, mobility))
    padded = extended(stacked, (("gx", 3), ("gy", 2)), 1)
    mob_near = padded[1]
    first = phase_field + step_size * laplace(padded[0], mob_near)
    first_pad = extended(first, (("gx", 2), ("gy", 1)), 1)
    second = (first + step_size * laplace(first_pad, mob_near)).astype(jnp.bfloat16)
    planes, y_rows, x_rows = second.shape
    out_rows = x_inverse.shape[0]
    segment = lax.all_gather(second, "gx", axis=2, tiled=True)
    flat = segment.reshape(planes * y_rows, segment.shape[2])
    lines = lax.dot_general(
        flat, x_inverse, (((1,), (1,)), ((), ())), preferred_element_type=jnp.float32
    )
    solved = lines.reshape(planes, y_rows, out_rows)
    chemical = solved * solved * solved - solved
    chemical_pad = extended(chemical, (("gx", 2), ("gy", 1)), 1)
    updated = (solved + step_size * laplace(chemical_pad, mob_near)).astype(jnp.bfloat16)
    columns = jnp.transpose(updated, (1, 0, 2)).reshape(y_rows, planes * x_rows)
    line_block = lax.all_to_all(columns, "gy", split_axis=1, concat_axis=0, tiled=True)
    solved_cols = jnp.dot(whole_inverse, line_block, preferred_element_type=jnp.float32)
    returned = lax.all_to_all(solved_cols, "gy", split_axis=0, concat_axis=1, tiled=True)
    return jnp.transpose(returned.reshape(y_rows, planes, x_rows), (1, 0, 2))


def half_mob(center_mob, near_mob):
    total = jnp.maximum(center_mob + near_mob, 0.25)
    inverse = pl.reciprocal(total, approx=True)
    inverse = inverse * (2.0 - total * inverse)
    return center_mob * near_mob * inverse


def sweep_plane(z, v, m, above, cols, chemical, y_rows, width, store):
    def flux_down(r, n):
        tall_v, tall_m = chemical(v[z, pl.ds(r, n + PAD), :]), m[z, pl.ds(r, n + PAD), :]
        low_v, low_m = pltpu.roll(tall_v, n + PAD - 1, 0)[:n], pltpu.roll(tall_m, n + PAD - 1, 0)[:n]
        return half_mob(tall_m[:n], low_m) * (low_v - tall_v[:n]), tall_v[:n], tall_m[:n]

    def strip(i, carried):
        r = pl.multiple_of(i * STRIP, STRIP)
        inner, mine = pl.ds(r + PAD, STRIP), pl.ds(r, STRIP)
        down, own, mob = flux_down(r + PAD, STRIP)
        stacked = jnp.concatenate([carried, down], axis=0)
        total = down - pltpu.roll(stacked, 1, 0)[PAD:]
        below = half_mob(mob, m[z + 1, inner, :]) * (chemical(v[z + 1, inner, :]) - own)
        total = total + (below - above[mine, :])
        above[mine, :] = below
        v_left, v_right, m_left, m_right = cols(z, mine)
        lane = lax.broadcasted_iota(jnp.int32, own.shape, 1)
        at_end = lane == width - 1
        v_next = jnp.where(at_end, v_right, pltpu.roll(own, width - 1, 1))
        m_next = jnp.where(at_end, m_right, pltpu.roll(mob, width - 1, 1))
        flux = half_mob(mob, m_next) * (v_next - own)
        entering = half_mob(m_left, mob[:, 0:1]) * (own[:, 0:1] - v_left)
        total = total + (flux - jnp.where(lane == 0, entering, pltpu.roll(flux, 1, 1)))
        store(mine, inner, total)
        return down[STRIP - PAD:]

    first_carry, _, _ = flux_down(0, PAD)
    lax.fori_loop(0, y_rows // STRIP, strip, first_carry)


def step_kernel(
    nx, ny, stages, w,
    phase, mobility, x_hbm, y_hbm, out, gath,
    v, m, f, second, gbuf, xsrc, xt, yinv, upd, yrecv, above1, above2, above3, e1, r1, e2, r2,
    load_sems, in_sems, row_send, row_recv, f_send, f_recv, col_send, col_recv, xr_send, xr_recv,
    y_send, y_recv, gx_send, gx_recv, pair_send, pair_recv, sol_send, sol_recv,
    a2a_send, a2a_recv, ret_send, ret_recv, keep_sems, g_sems,
):
    planes, y_rows, width = phase.shape
    gx, gy = lax.axis_index("gx"), lax.axis_index("gy")
    partner = gx + 1 - 2 * lax.rem(gx, 2)
    mate = gy + 1 - 2 * lax.rem(gy, 2)
    side_half = lax.rem(gx, 2)
    half, y_half = nx // 2, ny // 2
    per = len(stages)
    chunk = planes // per
    cuts = width // w
    depth = y_rows // 2
    every = pl.ds(0, planes)

    def remote(src, dst, send, recv, x_to, y_to):
        return pltpu.make_async_remote_copy(
            src, dst, send, recv, device_id=(x_to, y_to), device_id_type=MESH)

    barrier = pltpu.get_barrier_semaphore()
    for d in range(1, ny):
        pl.semaphore_signal(barrier, inc=1, device_id=(gx, lax.rem(gy + d, ny)), device_id_type=MESH)
    for d in range(1, nx):
        pl.semaphore_signal(barrier, inc=1, device_id=(lax.rem(gx + d, nx), gy), device_id_type=MESH)

    loads = [
        pltpu.make_async_copy(x_hbm, xsrc.at[pl.ds(0, width), :], load_sems.at[0]),
        pltpu.make_async_copy(y_hbm.at[pl.ds(0, depth), :], yinv.at[gy, 0], load_sems.at[1]),
        pltpu.make_async_copy(y_hbm.at[pl.ds(depth, depth), :], yinv.at[gy, 1], load_sems.at[2]),
    ]
    def load(g):
        group = pl.ds(g * chunk, chunk)
        return (pltpu.make_async_copy(phase.at[group], v.at[group, pl.ds(PAD, y_rows), :], in_sems.at[g, 0]),
                pltpu.make_async_copy(mobility.at[group], m.at[group, pl.ds(PAD, y_rows), :], in_sems.at[g, 1]))

    for g in range(per):
        for copy in load(g):
            copy.start()
    for copy in loads:
        copy.start()

    up_ok, down_ok = gy > 0, gy < ny - 1
    left_ok, right_ok = gx > 0, gx < nx - 1

    @pl.when(gy == 0)
    def _():
        for ref in (v, m, f):
            ref[every, pl.ds(0, PAD), :] = jnp.zeros((planes, PAD, width), jnp.float32)

    @pl.when(gy == ny - 1)
    def _():
        for ref in (v, m, f):
            ref[every, pl.ds(PAD + y_rows, PAD), :] = jnp.zeros((planes, PAD, width), jnp.float32)

    @pl.when(gx == 0)
    def _():
        r1[0] = jnp.zeros(r1.shape[1:], jnp.float32)
        for g in range(per):
            r2[g, 0] = jnp.zeros(r1.shape[1:], jnp.float32)
        xsrc[pl.ds(width, 16), :] = jnp.zeros((16, xsrc.shape[1]), xsrc.dtype)

    @pl.when(gx == nx - 1)
    def _():
        r1[1] = jnp.zeros(r1.shape[1:], jnp.float32)
        for g in range(per):
            r2[g, 1] = jnp.zeros(r1.shape[1:], jnp.float32)
        xsrc[pl.ds(width + 16, 16), :] = jnp.zeros((16, xsrc.shape[1]), xsrc.dtype)

    xsrc[pl.ds(width + 32, 96), :] = jnp.zeros((96, xsrc.shape[1]), xsrc.dtype)
    pl.semaphore_wait(barrier, ny - 1 + nx - 1)

    def edge_rows(src, lead, dst, lo, n, k, sends, recvs):
        planes_of = pl.ds(lo, n)
        down = remote(src.at[planes_of, pl.ds(lead + y_rows - PAD, PAD), :], dst.at[planes_of, pl.ds(0, PAD), :],
                      sends.at[k, 0], recvs.at[k, 0], gx, lax.rem(gy + 1, ny))
        up = remote(src.at[planes_of, pl.ds(lead, PAD), :], dst.at[planes_of, pl.ds(PAD + y_rows, PAD), :],
                    sends.at[k, 1], recvs.at[k, 1], gx, lax.rem(gy + ny - 1, ny))
        return down, up

    def columns(src, dst, k):
        right = remote(src.at[0], dst.at[0], col_send.at[k, 0], col_recv.at[k, 0], lax.rem(gx + 1, nx), gy)
        left = remote(src.at[1], dst.at[1], col_send.at[k, 1], col_recv.at[k, 1], lax.rem(gx + nx - 1, nx), gy)
        return right, left

    def inverse_rows():
        right = remote(x_hbm.at[pl.ds(width - 16, 16), :], xsrc.at[pl.ds(width, 16), :],
                       xr_send.at[0], xr_recv.at[0], lax.rem(gx + 1, nx), gy)
        left = remote(x_hbm.at[pl.ds(0, 16), :], xsrc.at[pl.ds(width + 16, 16), :],
                      xr_send.at[1], xr_recv.at[1], lax.rem(gx + nx - 1, nx), gy)
        return right, left

    def both(pair, ok_after, ok_before, act_after, act_before):
        @pl.when(ok_after)
        def _():
            act_on(pair[0], act_after)

        @pl.when(ok_before)
        def _():
            act_on(pair[1], act_before)

    def act_on(copy, act):
        if act == 0:
            copy.start()
        elif act == 1:
            copy.wait_send()
        else:
            copy.wait_recv()

    def start_rows(pair):
        both(pair, down_ok, up_ok, 0, 0)

    def sent_rows(pair):
        both(pair, down_ok, up_ok, 1, 1)

    def got_rows(pair):
        both(pair, up_ok, down_ok, 2, 2)

    def start_cols(pair):
        both(pair, right_ok, left_ok, 0, 0)

    def sent_cols(pair):
        both(pair, right_ok, left_ok, 1, 1)

    def got_cols(pair):
        both(pair, left_ok, right_ok, 2, 2)

    m_rows = edge_rows(mobility, 0, m, 0, planes, 0, row_send, row_recv)
    v_rows = edge_rows(phase, 0, v, 0, planes, 1, row_send, row_recv)
    start_rows(m_rows)
    start_rows(v_rows)
    start_cols(inverse_rows())

    def y_own(d):
        return remote(y_hbm.at[pl.ds(pl.multiple_of(side_half * depth, depth), depth), :], yinv.at[gy, side_half],
                      y_send.at[0, d], y_recv.at[0, d], gx, lax.rem(gy + 2 * d, ny))

    def y_arrived(d):
        slot = lax.rem(gy - 2 * d + ny, ny)
        return remote(yinv.at[slot, side_half], yinv.at[slot, side_half], y_send.at[0, d], y_recv.at[0, d],
                      gx, lax.rem(gy + 2 * d, ny))

    def y_mate(d):
        slot = lax.rem(gy - 2 * d + ny, ny)
        src = y_hbm.at[pl.ds(pl.multiple_of(side_half * depth, depth), depth), :] if d == 0 else yinv.at[slot, side_half]
        return remote(src, yinv.at[slot, side_half], y_send.at[1, d], y_recv.at[1, d], gx, mate)

    def y_from_mate(d):
        slot = lax.rem(mate - 2 * d + ny, ny)
        return remote(yinv.at[slot, side_half], yinv.at[slot, side_half], y_send.at[1, d], y_recv.at[1, d], gx, mate)

    def y_partner(k):
        slot = lax.rem(gy + k, ny)
        return remote(yinv.at[slot, side_half], yinv.at[slot, side_half], y_send.at[2, k], y_recv.at[2, k], partner, gy)

    def y_from_partner(k):
        slot = lax.rem(gy + k, ny)
        return remote(yinv.at[slot, 1 - side_half], yinv.at[slot, 1 - side_half], y_send.at[2, k], y_recv.at[2, k],
                      partner, gy)

    for ref in (v, m, f):
        ref[planes] = jnp.zeros(ref.shape[1:], jnp.float32)
    for ref in (above1, above2, above3):
        ref[...] = jnp.zeros_like(ref)

    pack_lane = lax.broadcasted_iota(jnp.int32, (y_rows, 128), 1)
    e1[...] = jnp.zeros_like(e1)
    e2[...] = jnp.zeros_like(e2)
    for g in range(per):
        for copy in load(g):
            copy.wait()

        @pl.loop(g * chunk, (g + 1) * chunk)
        def _(z):
            for ref, base in ((v, 0), (m, planes)):
                last = ref[z, pl.ds(PAD, y_rows), pl.ds(width - 128, 128)]
                lead = ref[z, pl.ds(PAD, y_rows), pl.ds(0, 128)]
                here = pack_lane == z + base
                e1[0] = jnp.where(here, last[:, 127:128], e1[0])
                e1[1] = jnp.where(here, lead[:, 0:1], e1[1])

    v_cols = columns(e1, r1, 0)
    start_cols(v_cols)

    loads[0].wait()
    got_cols(inverse_rows())
    for b in range(nx):
        xt[b] = xsrc[:, b * width:(b + 1) * width].T

    got_rows(m_rows)
    got_rows(v_rows)
    got_cols(v_cols)
    for d in range(1, y_half):
        y_own(d).start()
    y_mate(0).start()

    strip_lane = lax.broadcasted_iota(jnp.int32, (STRIP, 128), 1)

    def pick(ref, side, mine, at):
        return jnp.sum(jnp.where(strip_lane == at, ref[side, mine, :], 0.0), axis=1, keepdims=True)

    def plain_value(u):
        return u

    def chemical(u):
        return u * u * u - u

    def cols_from(ref):
        def cols(z, mine):
            return (pick(ref, 0, mine, z), pick(ref, 1, mine, z),
                    pick(r1, 0, mine, z + planes), pick(r1, 1, mine, z + planes))
        return cols

    def f_rows(s):
        lo, n = stages[s]
        return edge_rows(f, PAD, f, lo, n, s, f_send, f_recv)

    def f_cols(s):
        return columns(e2.at[s], r2.at[s], 1 + s)

    def make_first(s):
        lo, n = stages[s]
        beyond = lo + n

        @pl.loop(lo + (1 if s else 0), min(beyond + 1, planes))
        def _(z):
            def store(mine, inner, total):
                value = v[z, inner, :] + 2.0 * step_size * total
                f[z, inner, :] = value
                here = strip_lane == z
                t = s if beyond == planes else s + lax.div(z, beyond)
                e2[t, 0, mine, :] = jnp.where(here, value[:, width - 1:width], e2[t, 0, mine, :])
                e2[t, 1, mine, :] = jnp.where(here, value[:, 0:1], e2[t, 1, mine, :])

            sweep_plane(z, v, m, above1, cols_from(r1), plain_value, y_rows, width, store)

        start_rows(f_rows(s))
        start_cols(f_cols(s))

    def make_second(s):
        lo, n = stages[s]
        got_rows(f_rows(s))
        got_cols(f_cols(s))

        @pl.loop(lo, lo + n)
        def _(z):
            def store(mine, inner, total):
                second[z, mine, :] = (f[z, inner, :] + 2.0 * step_size * total).astype(second.dtype)

            sweep_plane(z, f, m, above2, cols_from(r2.at[s]), plain_value, y_rows, width, store)
            for d in range(1, half):
                across(z, d).start()
            to_pair(z, 0).start()

    def across(z, d):
        return remote(second.at[z], gath.at[gx, z], gx_send.at[z, d], gx_recv.at[z, d], lax.rem(gx + 2 * d, nx), gy)

    def arrived(z, d):
        slot = lax.rem(gx - 2 * d + nx, nx)
        return remote(second.at[z], gath.at[slot, z], gx_send.at[z, d], gx_recv.at[z, d], lax.rem(gx + 2 * d, nx), gy)

    def to_pair(z, d):
        slot = lax.rem(gx - 2 * d + nx, nx)
        src = second.at[z] if d == 0 else gath.at[slot, z]
        return remote(src, gath.at[slot, z], pair_send.at[z, d], pair_recv.at[z, d], partner, gy)

    def from_pair(z, d):
        slot = lax.rem(partner - 2 * d + nx, nx)
        return remote(second.at[z], gath.at[slot, z], pair_send.at[z, d], pair_recv.at[z, d], partner, gy)

    def forward(s):
        lo, n = stages[s]

        @pl.loop(lo, lo + n)
        def _(z):
            for d in range(1, half):
                arrived(z, d).wait_recv()
                to_pair(z, d).start()

    def home(s, owner):
        off = pl.multiple_of(lax.rem(owner, cuts) * w, w)
        return out.at[s * chunk + lax.div(owner, cuts), :, pl.ds(off, w)]

    def spread(s, d):
        peer = lax.rem(gy + d, ny)
        return remote(upd.at[s, peer], yrecv.at[s, gy], a2a_send.at[s, d], a2a_recv.at[s, d], gx, peer)

    def landed(s, d):
        return remote(upd.at[s, 0], yrecv.at[s, lax.rem(gy - d + ny, ny)], a2a_send.at[s, d], a2a_recv.at[s, d],
                      gx, lax.rem(gy + d, ny))

    def back(s, d):
        peer = lax.rem(gy + d, ny)
        return remote(upd.at[s, peer], home(s, gy), ret_send.at[s, d], ret_recv.at[s, d], gx, peer)

    def returned(s, d):
        return remote(upd.at[s, 0], home(s, lax.rem(gy - d + ny, ny)), ret_send.at[s, d], ret_recv.at[s, d],
                      gx, lax.rem(gy + d, ny))

    def keep_in(s):
        return pltpu.make_async_copy(upd.at[s, gy], yrecv.at[s, gy], keep_sems.at[0, s])

    def keep_out(s):
        return pltpu.make_async_copy(upd.at[s, gy], home(s, gy), keep_sems.at[1, s])

    def solved_rows(s):
        lo, n = stages[s]
        return edge_rows(v, PAD, v, lo, n, s, sol_send, sol_recv)

    def fetch(z, k):
        slot = lax.rem(z, 2)
        return pltpu.make_async_copy(gath.at[lax.rem(gx + k, nx), z], gbuf.at[slot, k - 1], g_sems.at[slot, k - 1])

    def edge_cols(z, mine):
        beyond = f[z, mine, pl.ds(0, 128)]
        return (chemical(beyond[:, 15:16]), chemical(beyond[:, 16:17]),
                pick(r1, 0, mine, z + planes), pick(r1, 1, mine, z + planes))

    def solve_x(s):
        lo, n = stages[s]
        sent_rows(f_rows(s))

        @pl.loop(lo, lo + n)
        def _(z):
            for d in range(half):
                from_pair(z, d).wait_recv()

        for k in range(1, nx):
            fetch(lo, k).start()

        @pl.loop(lo, lo + n)
        def _(z):
            @pl.when(z + 1 < lo + n)
            def _():
                for k in range(1, nx):
                    fetch(z + 1, k).start()

            total = jnp.dot(second[z], xt[gx], preferred_element_type=jnp.float32)
            for k in range(1, nx):
                fetch(z, k).wait()
                total = total + jnp.dot(
                    gbuf[lax.rem(z, 2), k - 1], xt[lax.rem(gx + k, nx)], preferred_element_type=jnp.float32)
            v[z, pl.ds(PAD, y_rows), :] = total[:, :width]
            f[z, pl.ds(0, y_rows), pl.ds(0, 128)] = total[:, width:]

        start_rows(solved_rows(s))
        got_rows(solved_rows(s))

        @pl.loop(s * chunk, (s + 1) * chunk)
        def _(z):
            def store(mine, inner, total):
                value = (v[z, inner, :] + 2.0 * step_size * total).astype(upd.dtype)
                for c in range(cuts):
                    upd[s, (z - s * chunk) * cuts + c, mine, :] = value[:, c * w:(c + 1) * w]

            sweep_plane(z, v, m, above3, edge_cols, chemical, y_rows, width, store)

        keep_in(s).start()

        @pl.loop(1, ny)
        def _(d):
            spread(s, d).start()

    def share_inverse():
        for d in range(y_half):
            y_from_mate(d).wait_recv()
        for k in range(1, ny):
            y_partner(k).start()

    def solve_y(s):
        if s == 0:
            loads[1].wait()
            loads[2].wait()
            for k in range(1, ny):
                y_from_partner(k).wait_recv()
        keep_in(s).wait()

        @pl.loop(1, ny)
        def _(d):
            landed(s, d).wait_recv()
            spread(s, d).wait_send()

        def block(d):
            peer = lax.rem(gy + d, ny)
            lines = yrecv[s].reshape(ny * y_rows, w)
            upd[s, peer] = jnp.dot(
                yinv[peer].reshape(y_rows, ny * y_rows), lines, preferred_element_type=jnp.float32).astype(upd.dtype)

        @pl.loop(1, ny)
        def _(d):
            block(d)
            back(s, d).start()

        block(0)
        keep_out(s).start()

    for s in range(per):
        make_first(s)
        make_second(s)
        if s == per - 2:
            forward(0)
            for d in range(1, y_half):
                y_arrived(d).wait_recv()
                y_mate(d).start()

    for s in range(per):
        solve_x(s)
        if s + 1 < per:
            forward(s + 1)
        if s == 1:
            share_inverse()
        if s > 0:
            solve_y(s - 1)
    solve_y(per - 1)

    for pair in (m_rows, v_rows):
        sent_rows(pair)
    for pair in [v_cols, inverse_rows()] + [f_cols(s) for s in range(per)]:
        sent_cols(pair)
    for d in range(1, y_half):
        y_own(d).wait_send()
    for d in range(y_half):
        y_mate(d).wait_send()
    for k in range(1, ny):
        y_partner(k).wait_send()
    @pl.loop(0, planes)
    def _(z):
        for d in range(1, half):
            across(z, d).wait_send()
        for d in range(half):
            to_pair(z, d).wait_send()

    for s in range(per):
        sent_rows(solved_rows(s))
        keep_out(s).wait()

        @pl.loop(1, ny)
        def _(d):
            back(s, d).wait_send()
            returned(s, d).wait_recv()


def local(per, phase_field, mobility, x_inverse, y_inverse):
    planes, y_rows, width = phase_field.shape
    nx, ny = lax.axis_size("gx"), lax.axis_size("gy")
    chunk = planes // per
    w = chunk * width // ny
    ends = [min((s + 1) * chunk + 1, planes) for s in range(per)]
    starts = [0] + ends[:-1]
    stages = [(lo, hi - lo) for lo, hi in zip(starts, ends)]
    f32, bf16, dma = jnp.float32, jnp.bfloat16, pltpu.SemaphoreType.DMA
    tall = pltpu.VMEM((planes + 1, y_rows + 2 * PAD, width), f32)
    edges = pltpu.VMEM((2, y_rows, 128), f32)
    staged_edges = pltpu.VMEM((per, 2, y_rows, 128), f32)
    above = pltpu.VMEM((y_rows, width), f32)
    any_spec = pl.BlockSpec(memory_space=pl.ANY)
    lines, _ = pl.pallas_call(
        functools.partial(step_kernel, nx, ny, stages, w),
        out_shape=(
            jax.ShapeDtypeStruct((planes, y_rows, width), bf16),
            jax.ShapeDtypeStruct((nx, planes, y_rows, width), bf16),
        ),
        in_specs=[any_spec] * 4,
        out_specs=(any_spec, any_spec),
        scratch_shapes=[
            tall, tall, tall,
            pltpu.VMEM((planes, y_rows, width), bf16),
            pltpu.VMEM((2, nx - 1, y_rows, width), bf16),
            pltpu.VMEM((width + 128, nx * width), bf16),
            pltpu.VMEM((nx, width, width + 128), bf16),
            pltpu.VMEM((ny, 2, y_rows // 2, ny * y_rows), bf16),
            pltpu.VMEM((per, ny, y_rows, w), bf16),
            pltpu.VMEM((per, ny, y_rows, w), bf16),
            above, above, above,
            edges, edges, staged_edges, staged_edges,
            dma((3,)), dma((per, 2)), dma((2, 2)), dma((2, 2)), dma((per, 2)), dma((per, 2)),
            dma((1 + per, 2)), dma((1 + per, 2)), dma((2,)), dma((2,)),
            dma((3, ny)), dma((3, ny)),
            dma((planes, nx // 2)), dma((planes, nx // 2)), dma((planes, nx // 2)), dma((planes, nx // 2)),
            dma((per, 2)), dma((per, 2)),
            dma((per, ny)), dma((per, ny)), dma((per, ny)), dma((per, ny)),
            dma((2, per)), dma((2, nx - 1)),
        ],
        compiler_params=pltpu.CompilerParams(
            collective_id=0, has_side_effects=True, vmem_limit_bytes=62 * 2**20),
        cost_estimate=pl.CostEstimate(
            flops=8400 * phase_field.size, bytes_accessed=40 * phase_field.size, transcendentals=0),
    )(phase_field, mobility, x_inverse, y_inverse)
    return lines.astype(jnp.float32)


def chunks(planes, y_rows, width, nx, ny):
    if nx % 2 or ny % 2 or nx < 4 or ny < 4 or y_rows % STRIP or width % 128 or planes > 64:
        return 0
    if 30 * planes * y_rows * width > 64 * 2**20:
        return 0
    for per in (4, 2):
        if planes % per == 0 and planes // per * width % ny == 0:
            w = planes // per * width // ny
            if w % 128 == 0 and width % w == 0:
                return per
    return 0


def solution(mesh):
    placed = (P(None, "gy", "gx"), P(None, "gy", "gx"), P("gx", None), P("gy", None))
    nx, ny = mesh.shape["gx"], mesh.shape["gy"]

    def step(phase_field, mobility, x_inverse, y_inverse):
        planes, rows, cols = phase_field.shape
        per = chunks(planes, rows // ny, cols // nx, nx, ny)
        body = functools.partial(local, per) if per else plain
        return jax.shard_map(
            body, mesh=mesh, in_specs=placed, out_specs=P(None, "gy", "gx"), check_vma=False
        )(phase_field, mobility, x_inverse, y_inverse)

    return step
```

```python
import functools

import jax
import jax.numpy as jnp
from jax import lax
from jax.experimental import pallas as pl
from jax.experimental.pallas import tpu as pltpu
from jax.sharding import PartitionSpec as P

step_size = 0.15
PAD = 8
STRIP = 32
LONG = 16
MESH = pl.DeviceIdType.MESH


def face_mob(center_mob, near_mob):
    return 2.0 * center_mob * near_mob / jnp.maximum(center_mob + near_mob, 0.25)


def extended(x, sides, width):
    for axis, dim in sides:
        size, length = (lax.axis_size(axis), x.shape[dim])
        up = [(i, (i + 1) % size) for i in range(size - 1)]
        down = [(j, i) for i, j in up]
        last = lax.slice_in_dim(x, length - width, length, axis=dim)
        leading = lax.slice_in_dim(x, 0, width, axis=dim)
        before = lax.ppermute(last, axis, up)
        after = lax.ppermute(leading, axis, down)
        x = jnp.concatenate([before, x, after], axis=dim)
    return x


def laplace(values, mobile):
    values_z = jnp.pad(values, ((1, 1), (0, 0), (0, 0)))
    mobile_z = jnp.pad(mobile, ((1, 1), (0, 0), (0, 0)))
    center = values[:, 1:-1, 1:-1]
    center_mob = mobile[:, 1:-1, 1:-1]
    pairs = [
        (values_z[2:, 1:-1, 1:-1], mobile_z[2:, 1:-1, 1:-1]),
        (values_z[:-2, 1:-1, 1:-1], mobile_z[:-2, 1:-1, 1:-1]),
        (values[:, 2:, 1:-1], mobile[:, 2:, 1:-1]),
        (values[:, :-2, 1:-1], mobile[:, :-2, 1:-1]),
        (values[:, 1:-1, 2:], mobile[:, 1:-1, 2:]),
        (values[:, 1:-1, :-2], mobile[:, 1:-1, :-2]),
    ]
    result = jnp.zeros_like(center)
    for near_val, near_mob in pairs:
        result = result + face_mob(center_mob, near_mob) * (near_val - center)
    return result


def plain(phase_field, mobility, x_inverse, y_inverse):
    whole_inverse = lax.all_gather(y_inverse, "gy", axis=0, tiled=True)
    stacked = jnp.stack((phase_field, mobility))
    padded = extended(stacked, (("gx", 3), ("gy", 2)), 1)
    mob_near = padded[1]
    first = phase_field + step_size * laplace(padded[0], mob_near)
    first_pad = extended(first, (("gx", 2), ("gy", 1)), 1)
    second = (first + step_size * laplace(first_pad, mob_near)).astype(jnp.bfloat16)
    planes, y_rows, x_rows = second.shape
    out_rows = x_inverse.shape[0]
    segment = lax.all_gather(second, "gx", axis=2, tiled=True)
    flat = segment.reshape(planes * y_rows, segment.shape[2])
    lines = lax.dot_general(
        flat, x_inverse, (((1,), (1,)), ((), ())), preferred_element_type=jnp.float32
    )
    solved = lines.reshape(planes, y_rows, out_rows)
    chemical = solved * solved * solved - solved
    chemical_pad = extended(chemical, (("gx", 2), ("gy", 1)), 1)
    updated = (solved + step_size * laplace(chemical_pad, mob_near)).astype(jnp.bfloat16)
    columns = jnp.transpose(updated, (1, 0, 2)).reshape(y_rows, planes * x_rows)
    line_block = lax.all_to_all(columns, "gy", split_axis=1, concat_axis=0, tiled=True)
    solved_cols = jnp.dot(whole_inverse, line_block, preferred_element_type=jnp.float32)
    returned = lax.all_to_all(solved_cols, "gy", split_axis=0, concat_axis=1, tiled=True)
    return jnp.transpose(returned.reshape(y_rows, planes, x_rows), (1, 0, 2))


def half_mob(center_mob, near_mob):
    total = jnp.maximum(center_mob + near_mob, 0.25)
    inverse = pl.reciprocal(total, approx=True)
    inverse = inverse * (2.0 - total * inverse)
    return center_mob * near_mob * inverse


def sweep_plane(z, v, m, above, cols, chemical, base, rows, n, width, store):
    def flux_down(r, n):
        tall_v, tall_m = chemical(v[z, pl.ds(r, n + PAD), :]), m[z, pl.ds(r, n + PAD), :]
        low_v, low_m = pltpu.roll(tall_v, n + PAD - 1, 0)[:n], pltpu.roll(tall_m, n + PAD - 1, 0)[:n]
        return half_mob(tall_m[:n], low_m) * (low_v - tall_v[:n]), tall_v[:n], tall_m[:n]

    def strip(i, carried):
        r = pl.multiple_of(i * n + base, PAD)
        inner = pl.ds(r, n)
        down, own, mob = flux_down(r, n)
        stacked = jnp.concatenate([carried, down], axis=0)
        total = down - pltpu.roll(stacked, 1, 0)[PAD:]
        below = half_mob(mob, m[z + 1, inner, :]) * (chemical(v[z + 1, inner, :]) - own)
        total = total + (below - above[inner, :])
        above[inner, :] = below
        v_left, v_right, m_left, m_right = cols(z, inner)
        lane = lax.broadcasted_iota(jnp.int32, own.shape, 1)
        at_end = lane == width - 1
        v_next = jnp.where(at_end, v_right, pltpu.roll(own, width - 1, 1))
        m_next = jnp.where(at_end, m_right, pltpu.roll(mob, width - 1, 1))
        flux = half_mob(mob, m_next) * (v_next - own)
        entering = half_mob(m_left, mob[:, 0:1]) * (own[:, 0:1] - v_left)
        total = total + (flux - jnp.where(lane == 0, entering, pltpu.roll(flux, 1, 1)))
        store(inner, pl.ds(pl.multiple_of(i * n, n), n), total)
        return down[n - PAD:]

    carry = flux_down(base - PAD, PAD)[0] if base else jnp.zeros((PAD, width), jnp.float32)
    lax.fori_loop(0, rows // n, strip, carry)


def step_kernel(
    nx, ny, stages, w,
    phase, mobility, x_hbm, y_hbm, out, gath,
    v, m, f, second, gbuf, xsrc, xt, yinv, upd, yrecv, above, e1, r1, e2, r2,
    load_sems, row_send, row_recv, col_send, col_recv, xr_send, xr_recv,
    y_send, y_recv, gx_send, gx_recv, pair_send, pair_recv,
    a2a_send, a2a_recv, ret_send, ret_recv, keep_sems, g_sems,
):
    planes, y_rows, width = phase.shape
    gx, gy = lax.axis_index("gx"), lax.axis_index("gy")
    partner = gx + 1 - 2 * lax.rem(gx, 2)
    mate = gy + 1 - 2 * lax.rem(gy, 2)
    side_half = lax.rem(gx, 2)
    half, y_half = nx // 2, ny // 2
    per = len(stages)
    chunk = planes // per
    cuts = width // w
    depth = y_rows // 2
    every = pl.ds(0, planes)
    tall = y_rows + 2 * PAD

    def remote(src, dst, send, recv, x_to, y_to):
        return pltpu.make_async_remote_copy(
            src, dst, send, recv, device_id=(x_to, y_to), device_id_type=MESH)

    barrier = pltpu.get_barrier_semaphore()
    for d in range(1, ny):
        pl.semaphore_signal(barrier, inc=1, device_id=(gx, lax.rem(gy + d, ny)), device_id_type=MESH)
    for d in range(1, nx):
        pl.semaphore_signal(barrier, inc=1, device_id=(lax.rem(gx + d, nx), gy), device_id_type=MESH)

    loads = [
        pltpu.make_async_copy(phase, v.at[every, pl.ds(PAD, y_rows), :], load_sems.at[0]),
        pltpu.make_async_copy(mobility, m.at[every, pl.ds(PAD, y_rows), :], load_sems.at[1]),
        pltpu.make_async_copy(x_hbm, xsrc.at[pl.ds(0, width), :], load_sems.at[2]),
        pltpu.make_async_copy(y_hbm.at[pl.ds(0, depth), :], yinv.at[gy, 0], load_sems.at[3]),
        pltpu.make_async_copy(y_hbm.at[pl.ds(depth, depth), :], yinv.at[gy, 1], load_sems.at[4]),
    ]
    for copy in loads:
        copy.start()

    up_ok, down_ok = gy > 0, gy < ny - 1
    left_ok, right_ok = gx > 0, gx < nx - 1

    @pl.when(gy == 0)
    def _():
        for ref in (v, m, f):
            ref[every, pl.ds(0, PAD), :] = jnp.zeros((planes, PAD, width), jnp.float32)

    @pl.when(gy == ny - 1)
    def _():
        for ref in (v, m, f):
            ref[every, pl.ds(PAD + y_rows, PAD), :] = jnp.zeros((planes, PAD, width), jnp.float32)

    @pl.when(gx == 0)
    def _():
        for ref in (r1, r2):
            ref[0] = jnp.zeros(ref.shape[1:], jnp.float32)
        xsrc[pl.ds(width, 16), :] = jnp.zeros((16, xsrc.shape[1]), xsrc.dtype)

    @pl.when(gx == nx - 1)
    def _():
        for ref in (r1, r2):
            ref[1] = jnp.zeros(ref.shape[1:], jnp.float32)
        xsrc[pl.ds(width + 16, 16), :] = jnp.zeros((16, xsrc.shape[1]), xsrc.dtype)

    xsrc[pl.ds(width + 32, 96), :] = jnp.zeros((96, xsrc.shape[1]), xsrc.dtype)
    pl.semaphore_wait(barrier, ny - 1 + nx - 1)

    def edge_rows(src, lead, dst, lo, n, k, sends, recvs):
        planes_of = pl.ds(lo, n)
        down = remote(src.at[planes_of, pl.ds(lead + y_rows - PAD, PAD), :], dst.at[planes_of, pl.ds(0, PAD), :],
                      sends.at[k, 0], recvs.at[k, 0], gx, lax.rem(gy + 1, ny))
        up = remote(src.at[planes_of, pl.ds(lead, PAD), :], dst.at[planes_of, pl.ds(PAD + y_rows, PAD), :],
                    sends.at[k, 1], recvs.at[k, 1], gx, lax.rem(gy + ny - 1, ny))
        return down, up

    def columns(src, dst, k):
        right = remote(src.at[0], dst.at[0], col_send.at[k, 0], col_recv.at[k, 0], lax.rem(gx + 1, nx), gy)
        left = remote(src.at[1], dst.at[1], col_send.at[k, 1], col_recv.at[k, 1], lax.rem(gx + nx - 1, nx), gy)
        return right, left

    def inverse_rows():
        right = remote(x_hbm.at[pl.ds(width - 16, 16), :], xsrc.at[pl.ds(width, 16), :],
                       xr_send.at[0], xr_recv.at[0], lax.rem(gx + 1, nx), gy)
        left = remote(x_hbm.at[pl.ds(0, 16), :], xsrc.at[pl.ds(width + 16, 16), :],
                      xr_send.at[1], xr_recv.at[1], lax.rem(gx + nx - 1, nx), gy)
        return right, left

    def both(pair, ok_after, ok_before, act_after, act_before):
        @pl.when(ok_after)
        def _():
            act_on(pair[0], act_after)

        @pl.when(ok_before)
        def _():
            act_on(pair[1], act_before)

    def act_on(copy, act):
        if act == 0:
            copy.start()
        elif act == 1:
            copy.wait_send()
        else:
            copy.wait_recv()

    def start_rows(pair):
        both(pair, down_ok, up_ok, 0, 0)

    def sent_rows(pair):
        both(pair, down_ok, up_ok, 1, 1)

    def got_rows(pair):
        both(pair, up_ok, down_ok, 2, 2)

    def start_cols(pair):
        both(pair, right_ok, left_ok, 0, 0)

    def sent_cols(pair):
        both(pair, right_ok, left_ok, 1, 1)

    def got_cols(pair):
        both(pair, left_ok, right_ok, 2, 2)

    m_rows = edge_rows(mobility, 0, m, 0, planes, 0, row_send, row_recv)
    v_rows = edge_rows(phase, 0, v, 0, planes, 1, row_send, row_recv)
    start_rows(m_rows)
    start_rows(v_rows)
    start_cols(inverse_rows())

    def y_own(d):
        return remote(y_hbm.at[pl.ds(pl.multiple_of(side_half * depth, depth), depth), :], yinv.at[gy, side_half],
                      y_send.at[0, d], y_recv.at[0, d], gx, lax.rem(gy + 2 * d, ny))

    def y_arrived(d):
        slot = lax.rem(gy - 2 * d + ny, ny)
        return remote(yinv.at[slot, side_half], yinv.at[slot, side_half], y_send.at[0, d], y_recv.at[0, d],
                      gx, lax.rem(gy + 2 * d, ny))

    def y_mate(d):
        slot = lax.rem(gy - 2 * d + ny, ny)
        src = y_hbm.at[pl.ds(pl.multiple_of(side_half * depth, depth), depth), :] if d == 0 else yinv.at[slot, side_half]
        return remote(src, yinv.at[slot, side_half], y_send.at[1, d], y_recv.at[1, d], gx, mate)

    def y_from_mate(d):
        slot = lax.rem(mate - 2 * d + ny, ny)
        return remote(yinv.at[slot, side_half], yinv.at[slot, side_half], y_send.at[1, d], y_recv.at[1, d], gx, mate)

    def y_partner(k):
        slot = lax.rem(gy + k, ny)
        return remote(yinv.at[slot, side_half], yinv.at[slot, side_half], y_send.at[2, k], y_recv.at[2, k], partner, gy)

    def y_from_partner(k):
        slot = lax.rem(gy + k, ny)
        return remote(yinv.at[slot, 1 - side_half], yinv.at[slot, 1 - side_half], y_send.at[2, k], y_recv.at[2, k],
                      partner, gy)

    for ref in (v, m, f):
        ref[planes] = jnp.zeros(ref.shape[1:], jnp.float32)
        ref[every, pl.ds(tall, PAD), :] = jnp.zeros((planes, PAD, width), jnp.float32)
    above[...] = jnp.zeros_like(above)

    pack_lane = lax.broadcasted_iota(jnp.int32, (tall, 128), 1)
    e1[...] = jnp.zeros_like(e1)
    e2[...] = jnp.zeros_like(e2)
    loads[0].wait()
    loads[1].wait()
    got_rows(m_rows)
    got_rows(v_rows)
    for d in range(1, y_half):
        y_own(d).start()
    y_mate(0).start()

    @pl.loop(0, planes)
    def _(z):
        for ref, base in ((v, 0), (m, planes)):
            last = ref[z, pl.ds(0, tall), pl.ds(width - 128, 128)]
            lead = ref[z, pl.ds(0, tall), pl.ds(0, 128)]
            here = pack_lane == z + base
            e1[0] = jnp.where(here, last[:, 127:128], e1[0])
            e1[1] = jnp.where(here, lead[:, 0:1], e1[1])

    v_cols = columns(e1, r1, 0)
    f_cols = columns(e2, r2, 1)
    start_cols(v_cols)

    loads[2].wait()
    got_cols(inverse_rows())
    for b in range(nx):
        xt[b] = xsrc[:, b * width:(b + 1) * width].T

    got_cols(v_cols)

    def pick(ref, side, mine, at):
        packed = ref[side, mine, :]
        lane = lax.broadcasted_iota(jnp.int32, packed.shape, 1)
        return jnp.sum(jnp.where(lane == at, packed, 0.0), axis=1, keepdims=True)

    def plain_value(u):
        return u

    def chemical(u):
        return u * u * u - u

    def cols_from(ref):
        def cols(z, mine):
            return (pick(ref, 0, mine, z), pick(ref, 1, mine, z),
                    pick(r1, 0, mine, z + planes), pick(r1, 1, mine, z + planes))
        return cols

    @pl.loop(0, planes)
    def _(z):
        def store(mine, _, total):
            value = v[z, mine, :] + 2.0 * step_size * total
            f[z, mine, :] = value
            here = lax.broadcasted_iota(jnp.int32, (mine.size, 128), 1) == z
            e2[0, mine, :] = jnp.where(here, value[:, width - 1:width], e2[0, mine, :])
            e2[1, mine, :] = jnp.where(here, value[:, 0:1], e2[1, mine, :])

        sweep_plane(z, v, m, above, cols_from(r1), plain_value, 0, tall, LONG, width, store)

    start_cols(f_cols)
    above[...] = jnp.zeros_like(above)

    def across(s, d):
        lo, n = stages[s]
        return remote(second.at[pl.ds(lo, n)], gath.at[gx, pl.ds(lo, n)], gx_send.at[s, d], gx_recv.at[s, d],
                      lax.rem(gx + 2 * d, nx), gy)

    def arrived(s, d):
        lo, n = stages[s]
        slot = lax.rem(gx - 2 * d + nx, nx)
        return remote(second.at[pl.ds(lo, n)], gath.at[slot, pl.ds(lo, n)], gx_send.at[s, d], gx_recv.at[s, d],
                      lax.rem(gx + 2 * d, nx), gy)

    def to_pair(s, d):
        lo, n = stages[s]
        slot = lax.rem(gx - 2 * d + nx, nx)
        src = second.at[pl.ds(lo, n)] if d == 0 else gath.at[slot, pl.ds(lo, n)]
        return remote(src, gath.at[slot, pl.ds(lo, n)], pair_send.at[s, d], pair_recv.at[s, d], partner, gy)

    def from_pair(s, d):
        lo, n = stages[s]
        slot = lax.rem(partner - 2 * d + nx, nx)
        return remote(second.at[pl.ds(lo, n)], gath.at[slot, pl.ds(lo, n)], pair_send.at[s, d], pair_recv.at[s, d],
                      partner, gy)

    got_cols(f_cols)

    for s in range(per):
        lo, n = stages[s]

        @pl.loop(lo, lo + n)
        def _(z):
            def store(mine, _, total):
                second[z, mine, :] = (f[z, mine, :] + 2.0 * step_size * total).astype(second.dtype)

            sweep_plane(z, f, m, above, cols_from(r2), plain_value, 0, tall, LONG, width, store)

        for d in range(1, half):
            across(s, d).start()
        to_pair(s, 0).start()

    above[...] = jnp.zeros_like(above)
    for d in range(1, y_half):
        y_arrived(d).wait_recv()
        y_mate(d).start()

    def spread(s, d):
        peer = lax.rem(gy + d, ny)
        return remote(upd.at[s, peer], yrecv.at[s, gy], a2a_send.at[s, d], a2a_recv.at[s, d], gx, peer)

    def landed(s, d):
        return remote(upd.at[s, 0], yrecv.at[s, lax.rem(gy - d + ny, ny)], a2a_send.at[s, d], a2a_recv.at[s, d],
                      gx, lax.rem(gy + d, ny))

    def back(s, d):
        peer = lax.rem(gy + d, ny)
        return remote(upd.at[s, peer], out.at[s, gy], ret_send.at[s, d], ret_recv.at[s, d], gx, peer)

    def returned(s, d):
        return remote(upd.at[s, 0], out.at[s, lax.rem(gy - d + ny, ny)], ret_send.at[s, d], ret_recv.at[s, d],
                      gx, lax.rem(gy + d, ny))

    def keep_in(s):
        return pltpu.make_async_copy(upd.at[s, gy], yrecv.at[s, gy], keep_sems.at[0, s])

    def keep_out(s):
        return pltpu.make_async_copy(upd.at[s, gy], out.at[s, gy], keep_sems.at[1, s])

    def fetch(z, k):
        slot = lax.rem(z, 2)
        return pltpu.make_async_copy(gath.at[lax.rem(gx + k, nx), z], gbuf.at[slot, k - 1], g_sems.at[slot, k - 1])

    def edge_cols(z, mine):
        beyond = f[z, mine, pl.ds(0, 128)]
        return (chemical(beyond[:, 15:16]), chemical(beyond[:, 16:17]),
                pick(r1, 0, mine, z + planes), pick(r1, 1, mine, z + planes))

    def solve_x(s):
        lo, n = stages[s]
        for d in range(1, half):
            arrived(s, d).wait_recv()
            to_pair(s, d).start()
        for d in range(half):
            from_pair(s, d).wait_recv()
        for k in range(1, nx):
            fetch(lo, k).start()

        @pl.loop(lo, lo + n)
        def _(z):
            @pl.when(z + 1 < lo + n)
            def _():
                for k in range(1, nx):
                    fetch(z + 1, k).start()

            total = jnp.dot(second[z], xt[gx], preferred_element_type=jnp.float32)
            for k in range(1, nx):
                fetch(z, k).wait()
                total = total + jnp.dot(
                    gbuf[lax.rem(z, 2), k - 1], xt[lax.rem(gx + k, nx)], preferred_element_type=jnp.float32)
            v[z, pl.ds(0, tall), :] = total[:, :width]
            f[z, pl.ds(0, tall), pl.ds(0, 128)] = total[:, width:]


        @pl.loop(s * chunk, (s + 1) * chunk)
        def _(z):
            def store(inner, mine, total):
                value = (v[z, inner, :] + 2.0 * step_size * total).astype(upd.dtype)
                for c in range(cuts):
                    upd[s, (z - s * chunk) * cuts + c, mine, :] = value[:, c * w:(c + 1) * w]

            sweep_plane(z, v, m, above, edge_cols, chemical, PAD, y_rows, STRIP, width, store)

        keep_in(s).start()

        @pl.loop(1, ny)
        def _(d):
            spread(s, d).start()

    def share_inverse():
        for d in range(y_half):
            y_from_mate(d).wait_recv()
        for k in range(1, ny):
            y_partner(k).start()

    def solve_y(s):
        if s == 0:
            loads[3].wait()
            loads[4].wait()
            for k in range(1, ny):
                y_from_partner(k).wait_recv()
        keep_in(s).wait()

        @pl.loop(1, ny)
        def _(d):
            landed(s, d).wait_recv()
            spread(s, d).wait_send()

        def block(d):
            peer = lax.rem(gy + d, ny)
            lines = yrecv[s].reshape(ny * y_rows, w)
            upd[s, peer] = jnp.dot(
                yinv[peer].reshape(y_rows, ny * y_rows), lines, preferred_element_type=jnp.float32).astype(upd.dtype)

        @pl.loop(1, ny)
        def _(d):
            block(d)
            back(s, d).start()

        block(0)
        keep_out(s).start()

    for s in range(per):
        solve_x(s)
        if s == 0:
            share_inverse()
        else:
            solve_y(s - 1)
    solve_y(per - 1)

    for pair in (m_rows, v_rows):
        sent_rows(pair)
    for pair in (v_cols, f_cols, inverse_rows()):
        sent_cols(pair)
    for d in range(1, y_half):
        y_own(d).wait_send()
    for d in range(y_half):
        y_mate(d).wait_send()
    for k in range(1, ny):
        y_partner(k).wait_send()
    for s in range(per):
        for d in range(1, half):
            across(s, d).wait_send()
        for d in range(half):
            to_pair(s, d).wait_send()
        keep_out(s).wait()

        @pl.loop(1, ny)
        def _(d):
            back(s, d).wait_send()
            returned(s, d).wait_recv()


def local(per, phase_field, mobility, x_inverse, y_inverse):
    planes, y_rows, width = phase_field.shape
    nx, ny = lax.axis_size("gx"), lax.axis_size("gy")
    chunk = planes // per
    w = chunk * width // ny
    ends = [min((s + 1) * chunk + 1, planes) for s in range(per)]
    starts = [0] + ends[:-1]
    stages = [(lo, hi - lo) for lo, hi in zip(starts, ends)]
    f32, bf16, dma = jnp.float32, jnp.bfloat16, pltpu.SemaphoreType.DMA
    rows = y_rows + 2 * PAD
    tall = pltpu.VMEM((planes + 1, rows + PAD, width), f32)
    edges = pltpu.VMEM((2, rows, 128), f32)
    any_spec = pl.BlockSpec(memory_space=pl.ANY)
    lines, _ = pl.pallas_call(
        functools.partial(step_kernel, nx, ny, stages, w),
        out_shape=(
            jax.ShapeDtypeStruct((per, ny, y_rows, w), bf16),
            jax.ShapeDtypeStruct((nx, planes, rows, width), bf16),
        ),
        in_specs=[any_spec] * 4,
        out_specs=(any_spec, any_spec),
        scratch_shapes=[
            tall, tall, tall,
            pltpu.VMEM((planes, rows, width), bf16),
            pltpu.VMEM((2, nx - 1, rows, width), bf16),
            pltpu.VMEM((width + 128, nx * width), bf16),
            pltpu.VMEM((nx, width, width + 128), bf16),
            pltpu.VMEM((ny, 2, y_rows // 2, ny * y_rows), bf16),
            pltpu.VMEM((per, ny, y_rows, w), bf16),
            pltpu.VMEM((per, ny, y_rows, w), bf16),
            pltpu.VMEM((rows, width), f32),
            edges, edges, edges, edges,
            dma((5,)), dma((2, 2)), dma((2, 2)), dma((2, 2)), dma((2, 2)), dma((2,)), dma((2,)),
            dma((3, ny)), dma((3, ny)),
            dma((per, nx // 2)), dma((per, nx // 2)), dma((per, nx // 2)), dma((per, nx // 2)),
            dma((per, ny)), dma((per, ny)), dma((per, ny)), dma((per, ny)),
            dma((2, per)), dma((2, nx - 1)),
        ],
        compiler_params=pltpu.CompilerParams(
            collective_id=0, has_side_effects=True, vmem_limit_bytes=62 * 2**20),
        cost_estimate=pl.CostEstimate(
            flops=8400 * phase_field.size, bytes_accessed=40 * phase_field.size, transcendentals=0),
    )(phase_field, mobility, x_inverse, y_inverse)
    lines = lines.reshape(planes, width // w, y_rows, w)
    return jnp.transpose(lines, (0, 2, 1, 3)).reshape(planes, y_rows, width).astype(jnp.float32)


def chunks(planes, y_rows, width, nx, ny):
    if nx % 2 or ny % 2 or nx < 4 or ny < 4 or y_rows % STRIP or 2 * PAD % LONG or width % 128 or planes > 64:
        return 0
    if 30 * planes * y_rows * width > 64 * 2**20:
        return 0
    for per in (4, 2, 1):
        if planes % per == 0 and planes // per * width % ny == 0:
            w = planes // per * width // ny
            if w % 128 == 0 and width % w == 0:
                return per
    return 0


def solution(mesh):
    placed = (P(None, "gy", "gx"), P(None, "gy", "gx"), P("gx", None), P("gy", None))
    nx, ny = mesh.shape["gx"], mesh.shape["gy"]

    def step(phase_field, mobility, x_inverse, y_inverse):
        planes, rows, cols = phase_field.shape
        per = chunks(planes, rows // ny, cols // nx, nx, ny)
        body = functools.partial(local, per) if per else plain
        return jax.shard_map(
            body, mesh=mesh, in_specs=placed, out_specs=P(None, "gy", "gx"), check_vma=False
        )(phase_field, mobility, x_inverse, y_inverse)

    return step
```
